256 devices in a mesh: seq: 32 (over y_hi, z, core), head: 8 (over y_lo, x).
Axes of the slice: x: 4, y: 4 (y_hi: 2, y_lo: 2; y = y_hi * 2 + y_lo), z: 8, core: 2. Of those that a mesh axis runs over, the one named last changes fastest.
Arguments:
- queries: bfloat16 [4096, 2048], P('seq', 'head'), may hold values from -6 to 6
- keys: bfloat16 [4096, 2048], P('seq', 'head'), may hold values from -6 to 6
- values: bfloat16 [4096, 2048], P('seq', 'head'), may hold values from -6 to 6
- attn_out: bfloat16 [4096, 2048], P('seq', 'head'), may hold values from -6 to 6
- out_grad: bfloat16 [4096, 4096], P('seq', 'head'), may hold values from -6 to 6
- out_weight: bfloat16 [2048, 4096], P('head'), may hold values from -0.125 to 0.125
- segment_ids: int32 [4096], replicated, may hold values from 0 to 3, as said below
Outputs:
- query_grad: bfloat16 [4096, 2048], P('seq', 'head')
- key_grad: bfloat16 [4096, 2048], P('seq', 'head')
- value_grad: bfloat16 [4096, 2048], P('seq', 'head')
The draws below stay inside these ranges and needn't reach their ends.
Inputs may be any that keep to these rules, and one draw needn't show every extreme that they name: `segment_ids`: ids 0 to 3 never falling along the tokens; each of the 4 documents starts at a multiple of 16 tokens, and one of them is exactly 3072 tokens long.
All inputs are finite; a program needn't handle non-finite values.
Results may differ from the reference program's by a relative error of at most 0.0058.
Values may be sent and summed in bfloat16 or wider, within the bound.
A program may use at most 64 MiB of HBM per device.

```python
import math
import jax
import jax.numpy as jnp
from jax import lax

D = 4096
HEADS = 16
HD = 128
LEN = 4096
HW = 2048


def draw_queries(key, part):
    key = jax.random.fold_in(key, 21)
    result = jnp.clip(jax.random.normal(key, (LEN, HEADS * HD), jnp.float32), -6.0, 6.0)
    return result.astype(jnp.bfloat16)


def draw_keys(key, part):
    key = jax.random.fold_in(key, 33)
    result = jnp.clip(jax.random.normal(key, (LEN, HEADS * HD), jnp.float32), -6.0, 6.0)
    return result.astype(jnp.bfloat16)


def draw_segment_ids(key, part):
    key = jax.random.fold_in(key, 5)
    first_key, second_key, third_key = jax.random.split(key, 3)
    quarter = LEN // 64
    cut_one = jax.random.randint(first_key, (), 1, quarter)
    cut_two = jax.random.randint(second_key, (), 1, quarter - 1)
    cut_two = jnp.where(cut_two >= cut_one, cut_two + 1, cut_two)
    lower = jnp.minimum(cut_one, cut_two)
    upper = jnp.maximum(cut_one, cut_two)
    lengths = jnp.stack([jnp.asarray(3 * quarter, jnp.int32), lower, upper - lower, quarter - upper]).astype(jnp.int32)
    turned = jax.random.randint(third_key, (), 0, 4)
    lengths = jnp.roll(lengths, turned)
    bounds = jnp.cumsum(lengths) * 16
    positions = jnp.arange(LEN, dtype=jnp.int32)
    return jnp.sum((positions[:, None] >= bounds[None, :3]).astype(jnp.int32), axis=1).astype(jnp.int32)


def level_of(rng, shape, pieces, least, top_value):
    gain, own = 1.0, jax.random.fold_in(rng, 6)
    for dim, blocks in pieces:
        draws = jnp.exp(jax.random.uniform(jax.random.fold_in(own, dim), (blocks,), jnp.float32, least / len(pieces), top_value / len(pieces)))
        gain = gain * jnp.repeat(draws, shape[dim] // blocks).reshape([-1 if axis == dim else 1 for axis in range(len(shape))])
    return gain


def normal_values(own_key, shape, width, most, cuts=(), held_as=jnp.bfloat16):
    drawn = width * jax.random.normal(own_key, shape, jnp.float32)
    if cuts:
        drawn = drawn * level_of(own_key, shape, cuts, -0.22, 0.18)
    return jnp.clip(drawn, -most, most).astype(held_as)


def setup_inputs(seed: int = 0) -> dict:
    seeds = jax.random.split(jax.random.key(seed), 8)
    return {
        "queries": draw_queries(jax.random.fold_in(seeds[7], 71), 0),
        "keys": draw_keys(jax.random.fold_in(seeds[7], 71), 0),
        "values": normal_values(seeds[2], (LEN, HW), 1.0, 6.0, ((0, 32), (1, 8))),
        "attn_out": normal_values(seeds[3], (LEN, HW), 1.0, 6.0, ((0, 32), (1, 8))),
        "out_grad": normal_values(seeds[4], (LEN, D), 1.0, 6.0, ((0, 32), (1, 8))),
        "out_weight": normal_values(seeds[5], (HW, D), HW ** -0.5, 0.125, ((0, 8),)),
        "segment_ids": draw_segment_ids(jax.random.fold_in(seeds[7], 71), 0),
    }


def head_grads(query_head, key_head, value_head, grad_head, delta_head, segment_ids):
    block_rows = math.gcd(LEN, 1024)
    scaling = HD ** -0.5

    def query_block(carried, number):
        key_total, value_total = carried
        offset = (number * block_rows).astype(jnp.int32)
        query_rows = lax.dynamic_slice_in_dim(query_head, offset, block_rows)
        grad_rows = lax.dynamic_slice_in_dim(grad_head, offset, block_rows)
        delta_rows = lax.dynamic_slice_in_dim(delta_head, offset, block_rows)
        segment_rows = lax.dynamic_slice_in_dim(segment_ids, offset, block_rows)
        scores = jnp.dot(query_rows, key_head.T, preferred_element_type=jnp.float32) * scaling
        allowed = segment_rows[:, None] == segment_ids[None, :]
        largest = jnp.max(jnp.where(allowed, scores, -1e30), axis=-1)
        centred = jnp.where(allowed, scores, largest[:, None]) - largest[:, None]
        log_sum = largest + jnp.log(jnp.sum(jnp.where(allowed, jnp.exp(centred), 0.0), axis=-1))
        lowered = jnp.where(allowed, scores, log_sum[:, None]) - log_sum[:, None]
        probs = jnp.where(allowed, jnp.exp(lowered), 0.0)
        prob_grad = jnp.dot(grad_rows, value_head.T, preferred_element_type=jnp.float32)
        score_grad = probs * (prob_grad - delta_rows[:, None])
        probs_low = probs.astype(jnp.bfloat16)
        score_low = (score_grad * scaling).astype(jnp.bfloat16)
        value_total = value_total + jnp.dot(probs_low.T, grad_rows, preferred_element_type=jnp.float32)
        key_total = key_total + jnp.dot(score_low.T, query_rows, preferred_element_type=jnp.float32)
        query_add = jnp.dot(score_low, key_head, preferred_element_type=jnp.float32)
        return (key_total, value_total), query_add

    empty = jnp.zeros((LEN, HD), jnp.float32)
    numbers = jnp.arange(LEN // block_rows, dtype=jnp.int32)
    (key_total, value_total), query_parts = lax.scan(query_block, (empty, empty), numbers)
    return query_parts.reshape(LEN, HD), key_total, value_total


def split_heads(array):
    return array.reshape(LEN, HEADS, HD).transpose(1, 0, 2)


def join_heads(array):
    return array.transpose(1, 0, 2).reshape(LEN, HEADS * HD).astype(jnp.bfloat16)


def reference(queries, keys, values, attn_out, out_grad, out_weight, segment_ids):
    grad_attn = jnp.dot(out_grad, out_weight.T, preferred_element_type=jnp.float32).astype(jnp.bfloat16)
    grad_split = split_heads(grad_attn)
    deltas = jnp.sum(grad_split.astype(jnp.float32) * split_heads(attn_out).astype(jnp.float32), axis=-1)

    def one_head(operands):
        return head_grads(operands[0], operands[1], operands[2], operands[3], operands[4], segment_ids)

    query_total, key_total, value_total = lax.map(
        one_head, (split_heads(queries), split_heads(keys), split_heads(values), grad_split, deltas))
    return join_heads(query_total), join_heads(key_total), join_heads(value_total)
```

```python
import jax
import jax.numpy as jnp
from jax import lax
from jax.experimental import pallas as pl
from jax.experimental.pallas import tpu as pltpu
from jax.sharding import PartitionSpec as P

HD = 128
TOK = 128
EXTRA = 16
ROWS = TOK + EXTRA
SCALE = HD ** -0.5
LOG2E = 1.4426950408889634
MASKED = -1e30
MESH = pl.DeviceIdType.MESH
BF = jnp.bfloat16
F32 = jnp.float32


def dot_nt(a, b):
    return lax.dot_general(a, b, (((1,), (1,)), ((), ())), preferred_element_type=F32)


def dot_nn(a, b):
    return lax.dot_general(a, b, (((1,), (0,)), ((), ())), preferred_element_type=F32)


def across(row):
    return jnp.broadcast_to(row, (128, 128)).T


def down(column):
    return jnp.broadcast_to(column, (128, 128)).T[0:1, :]


def pieces(x, count):
    out = []
    for _ in range(count):
        high = x.astype(BF).astype(F32)
        out.append(high)
        x = x - high
    return out


def stat_tile(rows, first):
    place = lax.broadcasted_iota(jnp.int32, (EXTRA, 128), 0)
    tile = jnp.zeros((EXTRA, 128), F32)
    for k, row in enumerate(rows):
        tile = jnp.where(place == first + k, jnp.broadcast_to(row, (EXTRA, 128)), tile)
    return tile


def kernel(
    q_ref, k_ref, v_ref, o_ref, og_ref, w_ref, seg_ref,
    dq_ref, dk_ref, dv_ref,
    kb, vqb, gb, ogb, sb, ga, ystage, yin, yout, segc, dlt, mb, lb, dqa, dka, dva,
    ky_s, ky_r, vy_s, vy_r, qy_s, qy_r, gy_s, gy_r, out_s, out_r,
    kz_s, kz_r, kc_s, kc_r, vz_s, vz_r, vc_s, vc_r, gz_s, gz_r, gc_s, gc_r, og_s, og_r,
):
    seq = lax.axis_index("seq")
    head = lax.axis_index("head")
    y = seq // 16
    z = (seq // 2) % 8
    c = seq % 2
    ylo = head // 4
    x = head % 4
    partner = (1 - y) * 16 + z * 2 + c
    sibling = y * 16 + z * 2 + (1 - c)
    right = y * 16 + ((z + 1) % 8) * 2 + c
    left = y * 16 + ((z + 7) % 8) * 2 + c
    mine = pl.ds(pl.multiple_of(y * HD, HD), HD)
    other = pl.ds(pl.multiple_of((1 - y) * HD, HD), HD)

    barrier = pltpu.get_barrier_semaphore()
    for peer in (partner, sibling, right, left):
        pl.semaphore_signal(barrier, inc=1, device_id={"seq": peer}, device_id_type=MESH)
    offsets = [(dy, dx) for dy in range(2) for dx in range(4) if dy or dx]
    for dy, dx in offsets:
        peer = ((ylo + dy) % 2) * 4 + (x + dx) % 4
        pl.semaphore_signal(barrier, inc=1, device_id={"head": peer}, device_id_type=MESH)
    pl.semaphore_wait(barrier, 4 + len(offsets))

    def to_seq(src, dst, ssem, rsem, device):
        return pltpu.make_async_remote_copy(
            src_ref=src, dst_ref=dst, send_sem=ssem, recv_sem=rsem,
            device_id={"seq": device}, device_id_type=MESH)

    def order(e):
        odd = e % 2
        return odd * ((e + 1) // 2) + (1 - odd) * ((8 - e // 2) % 8)

    def z_copy(buf, ssem, rsem, slot, u, rightward):
        there = (slot + 2 * rightward + 7) % 8
        device = y * 16 + ((z + 2 * rightward + 7) % 8) * 2 + c
        return to_seq(buf.at[slot, 0, u], buf.at[there, 0, u], ssem.at[rightward, slot, u],
                      rsem.at[there, u], device)

    def z_arrive(buf, ssem, rsem, slot, u):
        to_seq(buf.at[slot, 0, u], buf.at[slot, 0, u], ssem.at[0, slot, u], rsem.at[slot, u], right).wait_recv()

    def c_copy(buf, ssem, rsem, slot):
        return to_seq(buf.at[slot, 0], buf.at[slot, 1], ssem.at[slot], rsem.at[slot], sibling)

    kring = (kb, kz_s, kz_r, kc_s, kc_r)
    vring = (vqb, vz_s, vz_r, vc_s, vc_r)
    gring = (gb, gz_s, gz_r, gc_s, gc_r)

    def first(ring, u):
        buf, zs, zr, _, _ = ring
        z_copy(buf, zs, zr, 0, u, 1).start()
        z_copy(buf, zs, zr, 0, u, 0).start()

    def relay(ring, e):
        buf, zs, zr, cs, cr = ring
        slot = order(e)
        odd = e % 2
        main = 1 - odd
        z_arrive(buf, zs, zr, slot, main)

        @pl.when(e < 7)
        def _():
            z_copy(buf, zs, zr, slot, main, odd).start()

        z_arrive(buf, zs, zr, slot, odd)

        @pl.when(e < 5)
        def _():
            z_copy(buf, zs, zr, slot, odd, odd).start()

        c_copy(buf, cs, cr, slot).start()

    def settle(ring):
        buf, zs, zr, cs, cr = ring
        for u in range(2):
            for slot in range(0, 4 - u):
                z_copy(buf, zs, zr, slot, u, 1).wait_send()
            for k in range(0, 3 + u):
                z_copy(buf, zs, zr, (8 - k) % 8, u, 0).wait_send()

        def one(slot, carry):
            c_copy(buf, cs, cr, slot).wait_send()
            return carry

        lax.fori_loop(0, 8, one, 0)

    ky = to_seq(k_ref.at[:, other], kb.at[0, 0, 1], ky_s, ky_r, partner)
    vy = to_seq(v_ref.at[:, other], vqb.at[0, 0, 1, 0], vy_s, vy_r, partner)
    qy = to_seq(q_ref.at[:, other], vqb.at[0, 0, 1, 1], qy_s, qy_r, partner)
    ky.start()
    vy.start()
    qy.start()
    kb[0, 0, 0] = k_ref[:, mine]
    first(kring, 0)
    vqb[0, 0, 0, 0] = v_ref[:, mine]
    vqb[0, 0, 0, 1] = q_ref[:, mine]

    og_copies = []
    for n, (dy, dx) in enumerate(offsets):
        peer = ((ylo + dy) % 2) * 4 + (x + dx) % 4
        slot = dy * 4 + (4 - dx) % 4
        og_copies.append(pltpu.make_async_remote_copy(
            src_ref=og_ref, dst_ref=ogb.at[slot], send_sem=og_s.at[dy * 4 + dx], recv_sem=og_r.at[slot],
            device_id={"head": peer}, device_id_type=MESH))
    for copy in og_copies:
        copy.start()

    seg_own = seg_ref[pl.ds(seq, 1), :].astype(F32)
    seg_far = seg_ref[pl.ds(partner, 1), :].astype(F32)
    segc[0:128, :] = across(seg_own)
    segc[128:256, :] = across(seg_far)
    mb[...] = jnp.full(mb.shape, MASKED, F32)
    lb[...] = jnp.zeros(lb.shape, F32)
    dqa[...] = jnp.zeros(dqa.shape, F32)
    dka[...] = jnp.zeros(dka.shape, F32)
    dva[...] = jnp.zeros(dva.shape, F32)

    ky.wait_recv()
    first(kring, 1)
    c_copy(kb, kc_s, kc_r, 0).start()
    vy.wait_recv()
    qy.wait_recv()

    def seg_row(slot):
        zz = (z + 8 - slot) % 8
        rows = []
        for cc in range(2):
            for u in range(2):
                plane = y if u == 0 else 1 - y
                core = c if cc == 0 else 1 - c
                rows.append(seg_ref[pl.ds(plane * 16 + zz * 2 + core, 1), :].astype(F32))
        return jnp.concatenate(rows, axis=1)

    def columns(slot):
        return pl.ds(pl.multiple_of(slot * 512, 512), 512)

    def wide(tile):
        return jnp.concatenate([tile] * 4, axis=1)

    def have(ring, slot):
        buf, _, _, cs, cr = ring
        c_copy(buf, cs, cr, slot).wait_recv()

    def pass_a(e):
        slot = order(e)
        keys = kb[slot].reshape(512, HD)
        row = seg_row(slot)
        for half in range(2):
            part = pl.ds(half * 128, 128)
            s = dot_nt(vqb[0, 0, half, 1], keys)
            s = jnp.where(wide(segc[part, :]) == row, s, MASKED)
            sb[part, columns(slot)] = s
            top = jnp.maximum(jnp.maximum(s[:, 0:128], s[:, 128:256]), jnp.maximum(s[:, 256:384], s[:, 384:512]))
            mb[part, :] = jnp.maximum(mb[part, :], top)

    def pass_b(e):
        slot = order(e)
        for half in range(2):
            part = pl.ds(half * 128, 128)
            p = jnp.exp2((sb[part, columns(slot)] - wide(mb[part, :])) * (SCALE * LOG2E))
            sb[part, columns(slot)] = p
            lb[part, :] += (p[:, 0:128] + p[:, 128:256]) + (p[:, 256:384] + p[:, 384:512])

    def pass_c(e):
        slot = order(e)
        vals = vqb[slot, :, :, 0].reshape(512, HD)
        keys = kb[slot].reshape(512, HD)
        for half in range(2):
            part = pl.ds(half * 128, 128)
            dp = dot_nt(gb[0, 0, half, 0:128], vals)
            ds = sb[part, columns(slot)] * (dp - wide(dlt[part, :]))
            dqa[part, :] += dot_nn(ds.astype(BF), keys)

    def pass_k(e):
        slot = order(e)
        quer = vqb[slot, :, :, 1].reshape(512, HD)
        grad = gb[slot, :, :, 0:128].reshape(512, HD)
        row = seg_row(slot)
        deltas, logs = [], []
        for cc in range(2):
            for u in range(2):
                stats = gb[slot, cc, u, 128:144].astype(F32)
                deltas.append(stats[0:1] + stats[1:2])
                logs.append((stats[2:3] + stats[3:4]) + stats[4:5])
        deltas = jnp.concatenate(deltas, axis=1)
        logs = jnp.concatenate(logs, axis=1) * LOG2E
        for half in range(2):
            part = pl.ds(half * 128, 128)
            s = dot_nt(kb[0, 0, half], quer) * (SCALE * LOG2E) - logs
            p = jnp.exp2(jnp.where(wide(segc[part, :]) == row, s, MASKED))
            dva[part, :] += dot_nn(p.astype(BF), grad)
            dp = dot_nt(vqb[0, 0, half, 0], grad)
            ds = p * (dp - deltas)
            dka[part, :] += dot_nn(ds.astype(BF), quer)

    def make_grad():
        acc = None
        for slot in range(8):
            dy, dx = slot // 4, slot % 4
            block = ((ylo + dy) % 2) * 4 + (x + dx) % 4
            if slot:
                pltpu.make_async_remote_copy(
                    src_ref=og_ref, dst_ref=ogb.at[slot], send_sem=og_s.at[slot], recv_sem=og_r.at[slot],
                    device_id={"head": head}, device_id_type=MESH).wait_recv()
                part = ogb[slot]
            else:
                part = og_ref[...]
            term = dot_nt(part, w_ref[:, pl.ds(pl.multiple_of(block * 512, 512), 512)])
            acc = term if acc is None else acc + term
        ga[...] = acc.astype(BF)
        grad_far = ga[:, other]
        grad_own = ga[:, mine]
        far = (grad_far.astype(F32) * o_ref[:, other].astype(F32)).T
        own = grad_own.astype(F32) * o_ref[:, mine].astype(F32)
        far_row = jnp.sum(far, axis=0, keepdims=True)
        own_col = jnp.sum(own, axis=1, keepdims=True)
        ystage[0:128, :] = grad_far
        ystage[128:144, :] = stat_tile(pieces(far_row, 2), 0).astype(BF)
        to_seq(ystage, gb.at[0, 0, 1], gy_s, gy_r, partner).start()
        gb[0, 0, 0, 0:128] = grad_own
        dlt[0:128, :] = jnp.broadcast_to(own_col, (128, 128))

    def ring_step(e, carry):
        @pl.when(e >= 1)
        def _():
            relay(kring, e)

        @pl.when(e == 1)
        def _():
            first(vring, 0)
            first(vring, 1)
            c_copy(vqb, vc_s, vc_r, 0).start()

        @pl.when(e >= 3)
        def _():
            relay(vring, e - 2)

        @pl.when(e >= 1)
        def _():
            have(kring, order(e - 1))
            pass_a(e - 1)

        @pl.when(e == 6)
        def _():
            make_grad()

        return carry

    lax.fori_loop(0, 8, ring_step, 0)
    have(kring, order(7))
    pass_a(7)
    relay(vring, 6)
    top = jnp.max(mb[...], axis=1, keepdims=True)
    mb[...] = jnp.broadcast_to(top, mb.shape)

    def b_step(e, carry):
        pass_b(e)
        return carry

    lax.fori_loop(0, 8, b_step, 0)
    total = jnp.sum(lb[...], axis=1, keepdims=True)
    lb[...] = jnp.broadcast_to(SCALE / total, lb.shape)
    logs = top * SCALE + jnp.log(total)
    gb[0, 0, 0, 128:144] = (
        stat_tile(pieces(down(dlt[0:128, 0:1]), 2), 0)
        + stat_tile(pieces(down(logs[0:128]), 3), 2)
    ).astype(BF)
    first(gring, 0)
    to_seq(ystage, gb.at[0, 0, 1], gy_s, gy_r, partner).wait_recv()
    stats = gb[0, 0, 1, 128:144].astype(F32)
    dlt[128:256, :] = across(stats[0:1] + stats[1:2])
    gb[0, 0, 1, 128:144] = (stats + stat_tile(pieces(down(logs[128:256]), 3), 2)).astype(BF)
    first(gring, 1)
    c_copy(gb, gc_s, gc_r, 0).start()
    relay(vring, 7)

    def last_step(e, carry):
        @pl.when(e < 8)
        def _():
            relay(gring, e)

        have(vring, order(e - 1))
        pass_c(e - 1)
        have(gring, order(e - 1))
        pass_k(e - 1)
        return carry

    lax.fori_loop(1, 9, last_step, 0)

    results = (dqa[...] * lb[...], dka[...] * SCALE, dva[...])
    outs = []
    for n, value in enumerate(results):
        yout[n] = value[128:256].astype(BF)
        copy = to_seq(yout.at[n], yin.at[n], out_s.at[n], out_r.at[n], partner)
        copy.start()
        outs.append(copy)
    for n, (value, ref) in enumerate(zip(results, (dq_ref, dk_ref, dv_ref))):
        ref[:, mine] = value[0:128].astype(BF)
    for n, ref in enumerate((dq_ref, dk_ref, dv_ref)):
        outs[n].wait_recv()
        ref[:, other] = yin[n]

    for copy in (ky, vy, qy, *outs, *og_copies):
        copy.wait_send()
    to_seq(ystage, gb.at[0, 0, 1], gy_s, gy_r, partner).wait_send()
    for ring in (kring, vring, gring):
        settle(ring)


def shards(queries, keys, values, attn_out, out_grad, out_weight, segment_ids):
    vmem = pl.BlockSpec(memory_space=pltpu.VMEM)
    dma = pltpu.SemaphoreType.DMA
    out = jax.ShapeDtypeStruct((TOK, 2 * HD), BF)
    ring_sems = [dma((2, 8, 2)), dma((8, 2)), dma((8,)), dma((8,))]
    return pl.pallas_call(
        kernel,
        out_shape=(out, out, out),
        in_specs=[vmem] * 7,
        out_specs=(vmem, vmem, vmem),
        scratch_shapes=[
            pltpu.VMEM((8, 2, 2, TOK, HD), BF),
            pltpu.VMEM((8, 2, 2, 2, TOK, HD), BF),
            pltpu.VMEM((8, 2, 2, ROWS, HD), BF),
            pltpu.VMEM((8, TOK, 512), BF),
            pltpu.VMEM((256, 4096), F32),
            pltpu.VMEM((TOK, 2 * HD), BF),
            pltpu.VMEM((ROWS, HD), BF),
            pltpu.VMEM((3, TOK, HD), BF),
            pltpu.VMEM((3, TOK, HD), BF),
            pltpu.VMEM((256, HD), F32),
            pltpu.VMEM((256, HD), F32),
            pltpu.VMEM((256, HD), F32),
            pltpu.VMEM((256, HD), F32),
            pltpu.VMEM((256, HD), F32),
            pltpu.VMEM((256, HD), F32),
            pltpu.VMEM((256, HD), F32),
            dma, dma, dma, dma, dma, dma, dma, dma, dma((3,)), dma((3,)),
            *ring_sems, *ring_sems, *ring_sems,
            dma((8,)), dma((8,)),
        ],
        compiler_params=pltpu.CompilerParams(
            collective_id=0, has_side_effects=True, vmem_limit_bytes=40 * 1024 * 1024),
    )(queries, keys, values, attn_out, out_grad, out_weight, segment_ids.reshape(32, 128))


def solution(mesh):
    return jax.shard_map(
        shards,
        mesh=mesh,
        in_specs=(
            P("seq", "head"),
            P("seq", "head"),
            P("seq", "head"),
            P("seq", "head"),
            P("seq", "head"),
            P("head", None),
            P(),
        ),
        out_specs=(P("seq", "head"), P("seq", "head"), P("seq", "head")),
        check_vma=False,
    )
```

```python
import jax
import jax.numpy as jnp
from jax import lax
from jax.experimental import pallas as pl
from jax.experimental.pallas import tpu as pltpu
from jax.sharding import PartitionSpec as P

HD = 128
TOK = 128
EXTRA = 16
ROWS = TOK + EXTRA
SCALE = HD ** -0.5
LOG2E = 1.4426950408889634
MASKED = -1e30
FLOOR = -1e29
MESH = pl.DeviceIdType.MESH
BF = jnp.bfloat16
F32 = jnp.float32

SEQ_PEERS = (
    (0, -1, 0), (0, 1, 0), (0, 2, 0), (0, -2, 0), (0, -3, 0),
    (0, 0, 1), (0, 1, 1), (0, -1, 1), (0, 3, 1), (0, -3, 1), (0, -2, 1),
    (1, 0, 0), (1, 1, 0), (1, 0, 1), (1, 1, 1), (1, -1, 1),
)
HEAD_PEERS = tuple((dy, dx) for dy in range(2) for dx in range(4) if dy or dx)
QUERY_STEPS = ((0, -1, 2, -3), (0, 1, -2, 3))


def dot_nt(a, b):
    return lax.dot_general(a, b, (((1,), (1,)), ((), ())), preferred_element_type=F32)


def dot_nn(a, b):
    return lax.dot_general(a, b, (((1,), (0,)), ((), ())), preferred_element_type=F32)


def across(row):
    return jnp.broadcast_to(row, (128, 128)).T


def pieces(x, count):
    out = []
    for _ in range(count):
        high = x.astype(BF).astype(F32)
        out.append(high)
        x = x - high
    return out


def stat_tile(rows):
    place = lax.broadcasted_iota(jnp.int32, (EXTRA, 128), 0)
    tile = jnp.zeros((EXTRA, 128), F32)
    for k, row in enumerate(rows):
        tile = jnp.where(place == k, jnp.broadcast_to(row, (EXTRA, 128)), tile)
    return tile.astype(BF)


def kernel(
    q_hbm, k_hbm, v_hbm, o_hbm, og_hbm, w_hbm, seg_hbm,
    dq_hbm, dk_hbm, dv_hbm,
    qb, kb, vb, gb, ogb, ls_in, ls_out, w_ref, o_ref, seg_ref, segk, kt, pb, mb, ga, gstage,
    dka, dva, dq_out, dq_own, dq_in, dkv_out, dkv_in, res,
    w_sem, o_sem, seg_sem, og_sem, own_sem, res_sem,
    q_s, q_r, k_s, k_r, v_s, v_r, g_s, g_r, og_s, og_r, ls_s, ls_r, dq_s, dq_r, dkv_s, dkv_r,
):
    seq = lax.axis_index("seq")
    head = lax.axis_index("head")
    y = seq // 16
    z = (seq // 2) % 8
    c = seq % 2
    ylo = head // 4
    x = head % 4
    sgn = 1 - 2 * ((z + c) % 2)

    def cols(other_head):
        h = 1 - c if other_head else c
        return pl.ds(pl.multiple_of(h * HD, HD), HD)

    def device(dy, steps, dc):
        yy = (1 - y) if dy else y
        return yy * 16 + ((z + 8 + sgn * steps) % 8) * 2 + (c + dc) % 2

    def to_seq(src, dst, ssem, rsem, target):
        return pltpu.make_async_remote_copy(
            src_ref=src, dst_ref=dst, send_sem=ssem, recv_sem=rsem,
            device_id={"seq": target}, device_id_type=MESH)

    def to_head(src, dst, ssem, rsem, target):
        return pltpu.make_async_remote_copy(
            src_ref=src, dst_ref=dst, send_sem=ssem, recv_sem=rsem,
            device_id={"head": target}, device_id_type=MESH)

    local = [
        pltpu.make_async_copy(k_hbm.at[:, cols(0)], kb.at[0, 0, 0], own_sem.at[0]),
        pltpu.make_async_copy(q_hbm.at[:, cols(0)], qb.at[0, 0], own_sem.at[1]),
        pltpu.make_async_copy(v_hbm.at[:, cols(0)], vb.at[0, 0, 0], own_sem.at[2]),
        pltpu.make_async_copy(seg_hbm, seg_ref, seg_sem),
        pltpu.make_async_copy(og_hbm, ogb.at[0], og_sem),
        pltpu.make_async_copy(o_hbm, o_ref, o_sem),
        pltpu.make_async_copy(w_hbm, w_ref, w_sem),
    ]
    for copy in local:
        copy.start()

    barrier = pltpu.get_barrier_semaphore()
    for peer in SEQ_PEERS:
        pl.semaphore_signal(barrier, inc=1, device_id={"seq": device(*peer)}, device_id_type=MESH)
    for dy, dx in HEAD_PEERS:
        peer = ((ylo + dy) % 2) * 4 + (x + dx) % 4
        pl.semaphore_signal(barrier, inc=1, device_id={"head": peer}, device_id_type=MESH)
    pl.semaphore_wait(barrier, len(SEQ_PEERS) + len(HEAD_PEERS))

    sent = []

    def go(copy):
        copy.start()
        sent.append(copy)

    def spread_keys(src, buf, ss, rs):
        for cc in range(2):
            for dy in range(2):
                for dz in range(2):
                    if cc or dy or dz:
                        steps = (-dz if cc else dz)
                        go(to_seq(src.at[:, cols(cc)], buf.at[dy, dz, cc], ss.at[dy, dz, cc], rs.at[dy, dz, cc],
                                  device(dy, steps, cc)))

    spread_keys(k_hbm, kb, k_s, k_r)
    for cc in range(2):
        for d in range(4):
            if cc or d:
                go(to_seq(q_hbm.at[:, cols(cc)], qb.at[d, cc], q_s.at[d, cc], q_r.at[d, cc],
                          device(0, QUERY_STEPS[cc][d], cc)))
    for dy, dx in HEAD_PEERS:
        peer = ((ylo + dy) % 2) * 4 + (x + dx) % 4
        slot = dy * 4 + (4 - dx) % 4
        go(to_head(og_hbm, ogb.at[slot], og_s.at[dy * 4 + dx], og_r.at[slot], peer))
    spread_keys(v_hbm, vb, v_s, v_r)

    for copy in local:
        copy.wait()

    for dy in range(2):
        for dz in range(2):
            for cc in range(2):
                row = seg_ref[pl.ds(device(dy, dz, cc), 1), :].astype(F32)
                segk[dy * 4 + dz * 2 + cc] = across(row)

    def query_segments(d):
        rows = [seg_ref[pl.ds(device(0, -d, cc), 1), :].astype(F32) for cc in range(2)]
        return jnp.concatenate(rows, axis=1)

    def arrived(buf, rs, *at):
        to_seq(buf.at[at], buf.at[at], rs.at[at], rs.at[at], seq).wait_recv()

    def keys_arrived(buf, rs):
        for dy in range(2):
            for dz in range(2):
                for cc in range(2):
                    if cc or dy or dz:
                        arrived(buf, rs, dy, dz, cc)

    keys_arrived(kb, k_r)
    for dy in range(2):
        for dz in range(2):
            for cc in range(2):
                n = dy * 4 + dz * 2 + cc
                kt[:, n * 128:(n + 1) * 128] = kb[dy, dz, cc].astype(F32).T.astype(BF)

    def chunk(n):
        return n // 2, n % 2

    def queries_arrived(buf, rs, d):
        @pl.when(d > 0)
        def _():
            arrived(buf, rs, d, 0)

        arrived(buf, rs, d, 1)

    def owner(d, cc):
        return device(0, -d, cc)

    def score_step(d, carry):
        queries_arrived(qb, q_r, d)
        quer = qb[d].reshape(256, HD)
        row = query_segments(d)
        top = jnp.full((8, 256), FLOOR, F32)
        for n in range(4):
            dy, dz = chunk(n)
            s = dot_nt(kb[dy, dz].reshape(256, HD), quer)
            seg = segk[2 * n:2 * n + 2].reshape(256, 128)
            s = jnp.where(jnp.concatenate([seg, seg], axis=1) == row, s, MASKED)
            pb[d, n * 256:(n + 1) * 256] = s
            top = jnp.maximum(top, jnp.max(s.reshape(32, 8, 256), axis=0))
        top = jnp.max(top, axis=0, keepdims=True)
        total = jnp.zeros((8, 256), F32)
        for n in range(4):
            p = jnp.exp2((pb[d, n * 256:(n + 1) * 256] - top) * (SCALE * LOG2E))
            pb[d, n * 256:(n + 1) * 256] = p
            total = total + jnp.sum(p.reshape(32, 8, 256), axis=0)
        total = jnp.sum(total, axis=0, keepdims=True)
        mb[d] = jnp.broadcast_to(top * SCALE, (8, 256))
        logs = jnp.where(total > 0.0, top * SCALE + jnp.log(jnp.maximum(total, 1e-37)), MASKED)
        for cc in range(2):
            ls_out[d, cc] = jnp.broadcast_to(logs[:, cc * 128:(cc + 1) * 128], (8, 128))

        @pl.when(d > 0)
        def _():
            to_seq(ls_out.at[d, 0], ls_in.at[d, 0], ls_s.at[d, 0], ls_r.at[d, 0], owner(d, 0)).start()

        to_seq(ls_out.at[d, 1], ls_in.at[d, 1], ls_s.at[d, 1], ls_r.at[d, 1], owner(d, 1)).start()
        return carry

    lax.fori_loop(0, 4, score_step, 0)

    logs = []
    for cc in range(2):
        parts = []
        for d in range(4):
            if cc or d:
                arrived(ls_in, ls_r, d, cc)
                parts.append(ls_in[d, cc][0:1])
            else:
                parts.append(ls_out[0, 0][0:1])
        top = jnp.maximum(jnp.maximum(parts[0], parts[1]), jnp.maximum(parts[2], parts[3]))
        total = sum(jnp.exp(part - top) for part in parts)
        logs.append(top + jnp.log(total))

    acc = None
    for slot in range(8):
        block = ((ylo + slot // 4) % 2) * 4 + (x + slot) % 4
        if slot:
            to_head(og_hbm, ogb.at[slot], og_s.at[slot], og_r.at[slot], head).wait_recv()
        term = dot_nt(ogb[slot], w_ref[:, pl.ds(pl.multiple_of(block * 512, 512), 512)])
        acc = term if acc is None else acc + term
    ga[...] = acc.astype(BF)
    for cc in range(2):
        grad = ga[:, cols(cc)]
        delta = jnp.sum((grad.astype(F32) * o_ref[:, cols(cc)].astype(F32)).T, axis=0, keepdims=True)
        gstage[cc, 0:128] = grad
        gstage[cc, 128:144] = stat_tile(pieces(delta, 2) + pieces(logs[cc], 3))
    for d in range(4):
        for cc in range(2):
            if cc or d:
                go(to_seq(gstage.at[cc], gb.at[d, cc], g_s.at[d, cc], g_r.at[d, cc],
                          device(0, QUERY_STEPS[cc][d], cc)))
    gb[0, 0] = gstage[0]

    dka[...] = jnp.zeros(dka.shape, F32)
    dva[...] = jnp.zeros(dva.shape, F32)
    keys_arrived(vb, v_r)

    def grad_step(d, carry):
        queries_arrived(gb, g_r, d)
        quer = qb[d].reshape(256, HD)
        grad = gb[d, :, 0:128].reshape(256, HD)
        deltas, logs = [], []
        for cc in range(2):
            stats = gb[d, cc, 128:144].astype(F32)
            deltas.append(stats[0:1] + stats[1:2])
            logs.append((stats[2:3] + stats[3:4]) + stats[4:5])
        deltas = jnp.concatenate(deltas, axis=1)
        share = jnp.exp(mb[d][0:1] - jnp.concatenate(logs, axis=1))
        dqt = jnp.zeros((HD, 256), F32)
        for n in range(4):
            part = pl.ds(n * 256, 256)
            dy, dz = chunk(n)
            p = pb[d, part] * share
            dva[part] += dot_nn(p.astype(BF), grad)
            dp = dot_nt(vb[dy, dz].reshape(256, HD), grad)
            ds = (p * (dp - deltas)).astype(BF)
            dka[part] += dot_nn(ds, quer)
            dqt = dqt + dot_nn(kt[:, n * 256:(n + 1) * 256], ds)
        for cc in range(2):
            dq_out[d, cc] = dqt[:, cc * 128:(cc + 1) * 128].T.astype(BF)

        @pl.when(d > 0)
        def _():
            to_seq(dq_out.at[d, 0], dq_in.at[d, 0], dq_s.at[d, 0], dq_r.at[d, 0], owner(d, 0)).start()

        to_seq(dq_out.at[d, 1], dq_in.at[d, 1], dq_s.at[d, 1], dq_r.at[d, 1], owner(d, 1)).start()
        return carry

    lax.fori_loop(0, 4, grad_step, 0)

    for dy in (1, 0):
        for dz in (1, 0):
            for cc in (1, 0):
                n = dy * 4 + dz * 2 + cc
                dkv_out[dy, dz, cc, 0] = (dka[n * 128:(n + 1) * 128] * SCALE).astype(BF)
                dkv_out[dy, dz, cc, 1] = dva[n * 128:(n + 1) * 128].astype(BF)
                if n:
                    go(to_seq(dkv_out.at[dy, dz, cc], dkv_in.at[dy, dz, cc], dkv_s.at[dy, dz, cc],
                              dkv_r.at[dy, dz, cc], device(dy, dz, cc)))

    for cc in range(2):
        value = None
        for d in range(4):
            if cc or d:
                arrived(dq_in, dq_r, d, cc)
                part = dq_in[d, cc].astype(F32)
            else:
                part = dq_out[0, 0].astype(F32)
            value = part if value is None else value + part
        res[0, :, cols(cc)] = (value * SCALE).astype(BF)
    for cc in range(2):
        values = [dka[0:128] * SCALE, dva[0:128]] if cc == 0 else [None, None]
        for dy in range(2):
            for dz in range(2):
                if cc or dy or dz:
                    arrived(dkv_in, dkv_r, dy, dz, cc)
                    for a in range(2):
                        part = dkv_in[dy, dz, cc, a].astype(F32)
                        values[a] = part if values[a] is None else values[a] + part
        for a in range(2):
            res[1 + a, :, cols(cc)] = values[a].astype(BF)
    results = [pltpu.make_async_copy(res.at[n], ref, res_sem.at[n]) for n, ref in enumerate((dq_hbm, dk_hbm, dv_hbm))]
    for copy in results:
        copy.start()
    for copy in sent:
        copy.wait_send()
    for d in range(4):
        for cc in range(2):
            if cc or d:
                to_seq(ls_out.at[d, cc], ls_in.at[d, cc], ls_s.at[d, cc], ls_r.at[d, cc], owner(d, cc)).wait_send()
                to_seq(dq_out.at[d, cc], dq_in.at[d, cc], dq_s.at[d, cc], dq_r.at[d, cc], owner(d, cc)).wait_send()
    for copy in results:
        copy.wait()


def shards(queries, keys, values, attn_out, out_grad, out_weight, segment_ids):
    anywhere = pl.BlockSpec(memory_space=pl.ANY)
    dma = pltpu.SemaphoreType.DMA
    vmem = pltpu.VMEM
    out = jax.ShapeDtypeStruct((TOK, 2 * HD), BF)
    query_sems = [dma((4, 2))] * 2
    key_sems = [dma((2, 2, 2))] * 2
    return pl.pallas_call(
        kernel,
        out_shape=(out, out, out),
        in_specs=[anywhere] * 7,
        out_specs=(anywhere, anywhere, anywhere),
        scratch_shapes=[
            vmem((4, 2, TOK, HD), BF),
            vmem((2, 2, 2, TOK, HD), BF),
            vmem((2, 2, 2, TOK, HD), BF),
            vmem((4, 2, ROWS, HD), BF),
            vmem((8, TOK, 512), BF),
            vmem((4, 2, 8, 128), F32),
            vmem((4, 2, 8, 128), F32),
            vmem((256, 4096), BF),
            vmem((TOK, 2 * HD), BF),
            vmem((32, 128), jnp.int32),
            vmem((8, 128, 128), F32),
            vmem((HD, 1024), BF),
            vmem((4, 1024, 256), F32),
            vmem((4, 8, 256), F32),
            vmem((TOK, 2 * HD), BF),
            vmem((2, ROWS, HD), BF),
            vmem((1024, HD), F32),
            vmem((1024, HD), F32),
            vmem((4, 2, TOK, HD), BF),
            vmem((TOK, HD), F32),
            vmem((4, 2, TOK, HD), BF),
            vmem((2, 2, 2, 2, TOK, HD), BF),
            vmem((2, 2, 2, 2, TOK, HD), BF),
            vmem((3, TOK, 2 * HD), BF),
            dma, dma, dma, dma, dma((3,)), dma((3,)),
            *query_sems, *key_sems, *key_sems, *query_sems, dma((8,)), dma((8,)),
            *query_sems, *query_sems, *key_sems,
        ],
        compiler_params=pltpu.CompilerParams(
            collective_id=0, has_side_effects=True, vmem_limit_bytes=40 * 1024 * 1024),
    )(queries, keys, values, attn_out, out_grad, out_weight, segment_ids.reshape(32, 128))


def solution(mesh):
    return jax.shard_map(
        shards,
        mesh=mesh,
        in_specs=(
            P("seq", "head"),
            P("seq", "head"),
            P("seq", "head"),
            P("seq", "head"),
            P("seq", "head"),
            P("head", None),
            P(),
        ),
        out_specs=(P("seq", "head"), P("seq", "head"), P("seq", "head")),
        check_vma=False,
    )
```

```python
import jax
import jax.numpy as jnp
from jax import lax
from jax.experimental import pallas as pl
from jax.experimental.pallas import tpu as pltpu
from jax.sharding import PartitionSpec as P

HD = 128
TOK = 128
EXTRA = 16
HALF = TOK // 2
ROWS = HALF + EXTRA
SCALE = HD ** -0.5
LOG2E = 1.4426950408889634
MASKED = -1e30
FLOOR = -1e29
MESH = pl.DeviceIdType.MESH
BF = jnp.bfloat16
F32 = jnp.float32

SEQ_PEERS = (
    (0, -1, 0), (0, 1, 0), (0, 2, 0), (0, -2, 0), (0, -3, 0), (0, 3, 0),
    (0, 0, 1), (0, 1, 1), (0, -1, 1), (0, 3, 1), (0, -3, 1), (0, -2, 1),
    (1, 0, 0), (1, 1, 0), (1, 0, 1), (1, 1, 1), (1, -1, 1),
)
KEY_SLOTS = tuple((dy, dz, cc) for dy in range(2) for dz in range(2) for cc in range(2))
HEAD_PEERS = ((1, 0), (0, 1), (0, 2), (0, 3))
QUERY_STEPS = ((0, -1, 2, -3), (0, 1, -2, 3))
SHARE_STEPS = tuple(tuple(-d + QUERY_STEPS[d % 2][e] for e in range(4)) for d in range(4))


def dot_nt(a, b):
    return lax.dot_general(a, b, (((1,), (1,)), ((), ())), preferred_element_type=F32)


def dot_nn(a, b):
    return lax.dot_general(a, b, (((1,), (0,)), ((), ())), preferred_element_type=F32)


def across(row):
    return jnp.broadcast_to(row, (128, 128)).T


def pieces(x, count):
    out = []
    for _ in range(count):
        high = x.astype(BF).astype(F32)
        out.append(high)
        x = x - high
    return out


def stat_tile(rows):
    place = lax.broadcasted_iota(jnp.int32, (EXTRA, 128), 0)
    tile = jnp.zeros((EXTRA, 128), F32)
    for k, row in enumerate(rows):
        tile = jnp.where(place == k, jnp.broadcast_to(row, (EXTRA, 128)), tile)
    return tile.astype(BF)


def kernel(
    q_hbm, k_hbm, v_hbm, o_hbm, og_hbm, w_hbm, seg_hbm,
    dq_hbm, dk_hbm, dv_hbm,
    qb, kb, vb, gb, og_own, ogb, ls_in, ls_out, dl, dlt, w_ref, o_ref, seg_ref, segk, segq, kt, pb, mb, sh, ga,
    gstage, dka, dva, dqt, dq_out, dq_in, dkv_out, dkv_in, res,
    w_sem, o_sem, seg_sem, og_sem, own_sem, res_sem,
    q_s, q_r, k_s, k_r, v_s, v_r, g_s, g_r, og_s, og_r, ls_s, ls_r, dq_s, dq_r, dkv_s, dkv_r,
):
    seq = lax.axis_index("seq")
    head = lax.axis_index("head")
    y = seq // 16
    z = (seq // 2) % 8
    c = seq % 2
    ylo = head // 4
    x = head % 4
    sgn = 1 - 2 * ((z + c) % 2)

    def cols(other_head):
        h = 1 - c if other_head else c
        return pl.ds(pl.multiple_of(h * HD, HD), HD)

    def device(dy, steps, dc):
        yy = y + dy * (1 - 2 * y)
        return yy * 16 + ((z + 8 + sgn * steps) % 8) * 2 + (c + dc) % 2

    def to_seq(src, dst, ssem, rsem, target):
        return pltpu.make_async_remote_copy(
            src_ref=src, dst_ref=dst, send_sem=ssem, recv_sem=rsem,
            device_id={"seq": target}, device_id_type=MESH)

    def to_head(src, dst, ssem, rsem, target):
        return pltpu.make_async_remote_copy(
            src_ref=src, dst_ref=dst, send_sem=ssem, recv_sem=rsem,
            device_id={"head": target}, device_id_type=MESH)

    local = [
        pltpu.make_async_copy(k_hbm.at[:, cols(0)], kb.at[0, 0, 0], own_sem.at[0]),
        pltpu.make_async_copy(q_hbm.at[:, cols(0)], qb.at[0, 0], own_sem.at[1]),
        pltpu.make_async_copy(v_hbm.at[:, cols(0)], vb.at[0, 0, 0], own_sem.at[2]),
        pltpu.make_async_copy(og_hbm, og_own, og_sem),
        pltpu.make_async_copy(o_hbm, o_ref, o_sem),
        pltpu.make_async_copy(w_hbm, w_ref, w_sem),
    ]
    seg_copy = pltpu.make_async_copy(seg_hbm, seg_ref, seg_sem)
    seg_copy.start()
    for copy in local:
        copy.start()

    barrier = pltpu.get_barrier_semaphore()
    for peer in SEQ_PEERS:
        pl.semaphore_signal(barrier, inc=1, device_id={"seq": device(*peer)}, device_id_type=MESH)
    for dy, dx in HEAD_PEERS:
        peer = ((ylo + dy) % 2) * 4 + (x + dx) % 4
        pl.semaphore_signal(barrier, inc=1, device_id={"head": peer}, device_id_type=MESH)
    pl.semaphore_wait(barrier, len(SEQ_PEERS) + len(HEAD_PEERS))

    sent = []

    def go(copy):
        copy.start()
        sent.append(copy)

    def spread_keys(src, buf, ss, rs):
        for dy, dz, cc in ((1, 0, 0), (1, 0, 1), (0, 1, 0), (0, 1, 1), (0, 0, 1)):
            steps = (-dz if cc else dz)
            at = (dy, dz, cc)
            go(to_seq(src.at[:, cols(cc)], buf.at[at], ss.at[at], rs.at[at], device(dy, steps, cc)))

    def arrived(buf, rs, *at):
        to_seq(buf.at[at], buf.at[at], rs.at[at], rs.at[at], seq).wait_recv()

    def keys_on(buf, ss, rs):
        for cc in range(2):
            arrived(buf, rs, 1, 0, cc)
            go(to_seq(buf.at[1, 0, cc], buf.at[1, 1, cc], ss.at[1, 1, cc], rs.at[1, 1, cc], device(0, 1, 0)))

    def keys_arrived(buf, rs):
        for dy, dz, cc in ((0, 0, 1), (0, 1, 0), (0, 1, 1), (1, 1, 0), (1, 1, 1)):
            arrived(buf, rs, dy, dz, cc)

    def head_of(dy, dx):
        return ((ylo + dy) % 2) * 4 + (x + dx) % 4

    def rows_copy(src, slot, k, h, part, dy, dx):
        return to_head(src, ogb.at[slot, h, part], og_s.at[k, h, part], og_r.at[slot, h, part], head_of(dy, dx))

    def rows_to(*where):
        go(rows_copy(*where))

    def own_rows(h, part):
        n = h * 64 + part * 32
        return og_hbm.at[n:n + 32]

    def rows_x(h, part):
        for dx in (2, 1, 3):
            rows_to(own_rows(h, part), 4 - dx, dx, h, part, 0, dx)

    def rows_y(h, part):
        rows_to(own_rows(h, part), 4, 4, h, part, 1, 0)

    def rows_arrived(slot, h, part):
        at = (slot, h, part)
        to_head(ogb.at[at], ogb.at[at], og_s.at[at], og_r.at[at], head).wait_recv()

    def relay_x(h, dx):
        return rows_copy(ogb.at[4, h, 0], 8 - dx, 4 + dx, h, 0, 0, dx)

    def relay_y(h, dx):
        return rows_copy(ogb.at[dx, h, 1], 4 + dx, 4 + dx, h, 1, 1, 0)

    def rows_on_x(h):
        rows_arrived(4, h, 0)
        for dx in (2, 1, 3):
            relay_x(h, dx).start()

    def rows_on_y(h):
        for dx in (1, 3, 2):
            rows_arrived(dx, h, 1)
            relay_y(h, dx).start()

    def queries_to(*distances):
        for d in distances:
            for cc in range(2):
                if cc or d:
                    go(to_seq(q_hbm.at[:, cols(cc)], qb.at[d, cc], q_s.at[d, cc], q_r.at[d, cc],
                              device(0, QUERY_STEPS[cc][d], cc)))

    spread_keys(k_hbm, kb, k_s, k_r)
    rows_y(0, 0)
    rows_x(0, 1)
    rows_y(0, 1)
    rows_x(0, 0)
    rows_y(1, 0)
    rows_y(1, 1)
    rows_x(1, 1)
    queries_to(1, 0, 2, 3)
    seg_copy.wait()

    for dy in range(2):
        for dz in range(2):
            for cc in range(2):
                row = seg_ref[pl.ds(device(dy, dz, cc), 1), :].astype(F32)
                segk[dy * 4 + dz * 2 + cc] = across(row)

    for pair in range(2):
        rows = [seg_ref[pl.ds(device(0, -(2 * pair + dd), cc), 1), :].astype(F32) for dd in range(2) for cc in range(2)]
        for h in range(2):
            row = jnp.concatenate([r[:, h * 64:(h + 1) * 64] for r in rows], axis=1)
            segq[pair, h] = jnp.broadcast_to(row, (8, 256))

    def chunk(n):
        return n // 2, n % 2

    def blocks_arrived(buf, rs, pair, *lead):
        for dd in range(2):
            for cc in range(2):
                if dd or cc:
                    arrived(buf, rs, *lead, 2 * pair + dd, cc)
                else:
                    @pl.when(pair > 0)
                    def _():
                        arrived(buf, rs, *lead, 2 * pair, 0)

    def owner(d, cc):
        return device(0, -d, cc)

    def queries(pair, h):
        rows = pl.ds(pl.multiple_of(h * 64, 64), 64)
        return jnp.concatenate([qb[2 * pair + dd, cc, rows] for dd in range(2) for cc in range(2)], axis=0)

    mb[...] = jnp.full(mb.shape, FLOOR, F32)

    def scores(pair, dy):
        def one(h, carry):
            quer = queries(pair, h)
            row = segq[pair, h][0:1]
            top = mb[pair, h]
            for dz in range(2):
                n = 2 * dy + dz
                s = dot_nt(kb[dy, dz].reshape(256, HD), quer)
                seg = segk[2 * n:2 * n + 2].reshape(256, 128)
                s = jnp.where(jnp.concatenate([seg, seg], axis=1) == row, s, MASKED)
                pb[pair, h, n * 256:(n + 1) * 256] = s
                top = jnp.maximum(top, jnp.max(s.reshape(32, 8, 256), axis=0))
            mb[pair, h] = top
            return carry

        lax.fori_loop(0, 2, one, 0)

    for copy in local[:3]:
        copy.wait()
    rows_on_x(0)
    rows_on_y(0)
    rows_x(1, 0)
    keys_on(kb, k_s, k_r)
    for at in ((0, 0, 1), (0, 1, 0), (0, 1, 1)):
        arrived(kb, k_r, *at)
    blocks_arrived(qb, q_r, 0)
    scores(0, 0)
    rows_on_x(1)
    rows_on_y(1)
    spread_keys(v_hbm, vb, v_s, v_r)
    blocks_arrived(qb, q_r, 1)
    scores(1, 0)
    for cc in range(2):
        arrived(kb, k_r, 1, 1, cc)
    scores(0, 1)
    scores(1, 1)

    def share_copy(d, e):
        return to_seq(ls_out.at[d], ls_in.at[e, d], ls_s.at[d, e], ls_r.at[e, d], device(0, SHARE_STEPS[d][e], 0))

    for pair in range(2):
        def sum_step(h, carry):
            top = jnp.max(mb[pair, h], axis=0, keepdims=True)
            total = jnp.zeros((8, 256), F32)
            for n in range(4):
                p = jnp.exp2((pb[pair, h, n * 256:(n + 1) * 256] - top) * (SCALE * LOG2E))
                pb[pair, h, n * 256:(n + 1) * 256] = p
                total = total + jnp.sum(p.reshape(32, 8, 256), axis=0)
            total = jnp.sum(total, axis=0, keepdims=True)
            mb[pair, h] = jnp.broadcast_to(top * SCALE, (8, 256))
            logs = jnp.where(total > 0.0, top * SCALE + jnp.log(jnp.maximum(total, 1e-37)), MASKED)
            sh[pair, h] = jnp.broadcast_to(logs, (8, 256))
            return carry

        lax.fori_loop(0, 2, sum_step, 0)
        for dd in range(2):
            d = 2 * pair + dd
            for cc in range(2):
                n = (dd * 2 + cc) * 64
                ls_out[d, cc:cc + 1] = jnp.concatenate([sh[pair, 0][0:1, n:n + 64], sh[pair, 1][0:1, n:n + 64]], axis=1)
            for e in range(4):
                if e != d:
                    go(share_copy(d, e))
    for copy in local[3:]:
        copy.wait()

    def make_grad(h):
        acc = None
        for slot in (0, 4, 1, 3, 2, 5, 7, 6):
            block = ((ylo + slot // 4) % 2) * 4 + (x + slot) % 4
            for part in range(2):
                if slot and (slot, part) not in ((4, 0), (1, 1), (2, 1), (3, 1)):
                    rows_arrived(slot, h, part)
            rows = ogb[slot, h].reshape(HALF, 512) if slot else og_own[h * 64:(h + 1) * 64]
            term = dot_nt(rows, w_ref[:, pl.ds(pl.multiple_of(block * 512, 512), 512)])
            acc = term if acc is None else acc + term
        ga[h] = acc.astype(BF)
        for cc in range(2):
            grad = ga[h, :, cols(cc)]
            prod = grad.astype(F32) * o_ref[h * 64:(h + 1) * 64, cols(cc)].astype(F32)
            prod = jnp.concatenate([prod, jnp.zeros((64, HD), F32)], axis=0)
            gstage[h, cc, 0:HALF] = grad
            dl[h, cc] = jnp.broadcast_to(jnp.sum(prod.T, axis=0, keepdims=True), (8, 128))

    def send_grad(h):
        for cc in range(2):
            gstage[h, cc, HALF:ROWS] = stat_tile(pieces(dl[h, cc][0:1], 2))
        for d in (3, 2, 1, 0):
            for cc in range(2):
                if cc or d:
                    go(to_seq(gstage.at[h, cc], gb.at[h, d, cc], g_s.at[h, d, cc], g_r.at[h, d, cc],
                              device(0, QUERY_STEPS[cc][d], cc)))
        gb[h, 0, 0] = gstage[h, 0]

    make_grad(0)
    send_grad(0)
    keys_on(vb, v_s, v_r)
    make_grad(1)
    send_grad(1)
    for n, (dy, dz, cc) in enumerate(KEY_SLOTS):
        kt[:, n * 128:(n + 1) * 128] = kb[dy, dz, cc].astype(F32).T.astype(BF)
    dka[...] = jnp.zeros(dka.shape, F32)
    dva[...] = jnp.zeros(dva.shape, F32)
    keys_arrived(vb, v_r)
    log_sums = []
    for d in range(4):
        parts = [ls_out[d]]
        for e in range(4):
            if e != d:
                arrived(ls_in, ls_r, d, e)
                parts.append(ls_in[d, e])
        top = jnp.maximum(jnp.maximum(parts[0], parts[1]), jnp.maximum(parts[2], parts[3]))
        total = sum(jnp.exp(part - top) for part in parts)
        log_sums.append(top + jnp.log(total))
    for pair in range(2):
        for h in range(2):
            row = jnp.concatenate([
                log_sums[2 * pair + dd][cc:cc + 1, h * 64:(h + 1) * 64] for dd in range(2) for cc in range(2)], axis=1)
            sh[pair, h] = jnp.exp(mb[pair, h] - row)

    places = [(d, cc) for d in range(4) for cc in range(2)]

    def grad_step(i, carry):
        h, n = i // 4, 3 - i % 4
        dy, dz = n // 2, n % 2

        @pl.when(n == 3)
        def _():
            for d, cc in places:
                if d or cc:
                    arrived(gb, g_r, h, d, cc)
            dqt[...] = jnp.zeros(dqt.shape, F32)
            deltas = []
            for d, cc in places:
                stats = gb[h, d, cc, HALF:ROWS].astype(F32)
                deltas.append((stats[0:1] + stats[1:2])[:, 0:64])
            dlt[...] = jnp.broadcast_to(jnp.concatenate(deltas, axis=1), (8, 512))

        quer = jnp.concatenate([queries(pair, h) for pair in range(2)], axis=0)
        grad = jnp.concatenate([gb[h, d, cc, 0:HALF] for d, cc in places], axis=0)
        deltas = dlt[0:1]
        part = pl.ds(pl.multiple_of(n * 256, 256), 256)
        p = jnp.concatenate([pb[pair, h, part] * sh[pair, h][0:1] for pair in range(2)], axis=1)
        dva[part] += dot_nn(p.astype(BF), grad)
        dp = dot_nt(vb[dy, dz].reshape(256, HD), grad)
        ds = (p * (dp - deltas)).astype(BF)
        dka[part] += dot_nn(ds, quer)
        dqt[...] += dot_nn(kt[:, part], ds)

        @pl.when(h == 1)
        def _():
            for cc in range(2):
                rows = pl.ds(pl.multiple_of(n * 256 + cc * 128, 128), 128)
                dkv_out[dy, dz, cc, 0] = (dka[rows] * SCALE).astype(BF)
                dkv_out[dy, dz, cc, 1] = dva[rows].astype(BF)
                if cc:
                    dkv_copy(dy, dz, 1).start()
                else:
                    @pl.when(n > 0)
                    def _():
                        dkv_copy(dy, dz, 0).start()

        @pl.when(n == 0)
        def _():
            for d in (3, 2, 1, 0):
                tokens = dqt[:, d * 128:(d + 1) * 128].T.astype(BF)
                for cc in range(2):
                    dq_out[h, d, cc] = tokens[cc * 64:(cc + 1) * 64]
                    if d or cc:
                        dq_copy(h, d, cc).start()

        return carry

    def dq_copy(h, d, cc):
        return to_seq(dq_out.at[h, d, cc], dq_in.at[h, d, cc], dq_s.at[h, d, cc], dq_r.at[h, d, cc], owner(d, cc))

    def dkv_copy(dy, dz, cc):
        return to_seq(dkv_out.at[dy, dz, cc], dkv_in.at[dy, dz, cc], dkv_s.at[dy, dz, cc], dkv_r.at[dy, dz, cc],
                      device(dy, dz, cc))

    lax.fori_loop(0, 8, grad_step, 0)

    for h in range(2):
        for cc in range(2):
            value = None
            for d in range(4):
                if cc or d:
                    arrived(dq_in, dq_r, h, d, cc)
                    part = dq_in[h, d, cc].astype(F32)
                else:
                    part = dq_out[h, 0, 0].astype(F32)
                value = part if value is None else value + part
            res[0, h * 64:(h + 1) * 64, cols(cc)] = (value * SCALE).astype(BF)
    for cc in range(2):
        values = [dka[0:128] * SCALE, dva[0:128]] if cc == 0 else [None, None]
        for dy in range(2):
            for dz in range(2):
                if cc or dy or dz:
                    arrived(dkv_in, dkv_r, dy, dz, cc)
                    for a in range(2):
                        part = dkv_in[dy, dz, cc, a].astype(F32)
                        values[a] = part if values[a] is None else values[a] + part
        for a in range(2):
            res[1 + a, :, cols(cc)] = values[a].astype(BF)
    results = [pltpu.make_async_copy(res.at[n], ref, res_sem.at[n]) for n, ref in enumerate((dq_hbm, dk_hbm, dv_hbm))]
    for copy in results:
        copy.start()
    relays = [relay(h, dx) for h in range(2) for relay in (relay_x, relay_y) for dx in (1, 2, 3)]
    for copy in sent + relays:
        copy.wait_send()
    for d, cc in places:
        if cc or d:
            for h in range(2):
                dq_copy(h, d, cc).wait_send()
    for dy, dz, cc in KEY_SLOTS[1:]:
        dkv_copy(dy, dz, cc).wait_send()
    for copy in results:
        copy.wait()


def deliver(a_ref, b_ref, c_ref, dq_ref, dk_ref, dv_ref):
    dq_ref[...] = a_ref[...]
    dk_ref[...] = b_ref[...]
    dv_ref[...] = c_ref[...]


def shards(queries, keys, values, attn_out, out_grad, out_weight, segment_ids):
    anywhere = pl.BlockSpec(memory_space=pl.ANY)
    dma = pltpu.SemaphoreType.DMA
    vmem = pltpu.VMEM
    out = jax.ShapeDtypeStruct((TOK, 2 * HD), BF)
    query_sems = [dma((4, 2))] * 2
    key_sems = [dma((2, 2, 2))] * 2
    chunk_sems = [dma((2, 4, 2))] * 2
    held = pl.pallas_call(
        kernel,
        out_shape=(out, out, out),
        in_specs=[anywhere] * 7,
        out_specs=(anywhere, anywhere, anywhere),
        scratch_shapes=[
            vmem((4, 2, TOK, HD), BF),
            vmem((2, 2, 2, TOK, HD), BF),
            vmem((2, 2, 2, TOK, HD), BF),
            vmem((2, 4, 2, ROWS, HD), BF),
            vmem((TOK, 512), BF),
            vmem((8, 2, 2, 32, 512), BF),
            vmem((4, 4, 2, 128), F32),
            vmem((4, 2, 128), F32),
            vmem((2, 2, 8, 128), F32),
            vmem((8, 512), F32),
            vmem((256, 4096), BF),
            vmem((TOK, 2 * HD), BF),
            vmem((32, 128), jnp.int32),
            vmem((8, 128, 128), F32),
            vmem((2, 2, 8, 256), F32),
            vmem((HD, 1024), BF),
            vmem((2, 2, 1024, 256), F32),
            vmem((2, 2, 8, 256), F32),
            vmem((2, 2, 8, 256), F32),
            vmem((2, HALF, 2 * HD), BF),
            vmem((2, 2, ROWS, HD), BF),
            vmem((1024, HD), F32),
            vmem((1024, HD), F32),
            vmem((HD, 512), F32),
            vmem((2, 4, 2, HALF, HD), BF),
            vmem((2, 4, 2, HALF, HD), BF),
            vmem((2, 2, 2, 2, TOK, HD), BF),
            vmem((2, 2, 2, 2, TOK, HD), BF),
            vmem((3, TOK, 2 * HD), BF),
            dma, dma, dma, dma, dma((3,)), dma((3,)),
            *query_sems, *key_sems, *key_sems, *chunk_sems, dma((8, 2, 2)), dma((8, 2, 2)),
            dma((4, 4)), dma((4, 4)), *chunk_sems, *key_sems,
        ],
        compiler_params=pltpu.CompilerParams(
            collective_id=0, has_side_effects=True, vmem_limit_bytes=60 * 1024 * 1024),
    )(queries, keys, values, attn_out, out_grad, out_weight, segment_ids.reshape(32, 128))
    return pl.pallas_call(
        deliver,
        out_shape=(out, out, out),
        in_specs=[pl.BlockSpec(memory_space=pltpu.VMEM)] * 3,
        out_specs=(pl.BlockSpec(memory_space=pltpu.VMEM),) * 3,
        name="deliver_call",
    )(*held)


def solution(mesh):
    return jax.shard_map(
        shards,
        mesh=mesh,
        in_specs=(
            P("seq", "head"),
            P("seq", "head"),
            P("seq", "head"),
            P("seq", "head"),
            P("seq", "head"),
            P("head", None),
            P(),
        ),
        out_specs=(P("seq", "head"), P("seq", "head"), P("seq", "head")),
        check_vma=False,
    )
```

```python
import jax
import jax.numpy as jnp
from jax import lax
from jax.experimental import pallas as pl
from jax.experimental.pallas import tpu as pltpu
from jax.sharding import PartitionSpec as P

HD = 128
TOK = 128
EXTRA = 16
SPLIT = 64
PARTS = (slice(0, SPLIT), slice(SPLIT, TOK))
ROWS = TOK + EXTRA
SCALE = HD ** -0.5
LOG2E = 1.4426950408889634
MASKED = -1e30
FLOOR = -1e29
MESH = pl.DeviceIdType.MESH
BF = jnp.bfloat16
F32 = jnp.float32

SEQ_PEERS = (
    (0, -1, 0), (0, 1, 0), (0, 2, 0), (0, -2, 0), (0, -3, 0), (0, 3, 0),
    (0, 0, 1), (0, 1, 1), (0, -1, 1), (0, 3, 1), (0, -3, 1), (0, -2, 1),
    (1, 0, 0), (1, 1, 0), (1, 0, 1), (1, 1, 1), (1, -1, 1),
)
NEAR_FIRST = (1, 0, 2, 3)
KEY_SLOTS = tuple((dy, dz, cc) for dy in range(2) for dz in range(2) for cc in range(2))
HEAD_PEERS = ((1, 0), (0, 1), (0, 2), (0, 3))
QUERY_STEPS = ((0, -1, 2, -3), (0, 1, -2, 3))
SHARE_STEPS = tuple(tuple(-d + QUERY_STEPS[d % 2][e] for e in range(4)) for d in range(4))


def dot_nt(a, b):
    return lax.dot_general(a, b, (((1,), (1,)), ((), ())), preferred_element_type=F32)


def dot_nn(a, b):
    return lax.dot_general(a, b, (((1,), (0,)), ((), ())), preferred_element_type=F32)


def across(row):
    return jnp.broadcast_to(row, (128, 128)).T


def pieces(x, count):
    out = []
    for _ in range(count):
        high = x.astype(BF).astype(F32)
        out.append(high)
        x = x - high
    return out


def stat_tile(rows):
    place = lax.broadcasted_iota(jnp.int32, (EXTRA, 128), 0)
    tile = jnp.zeros((EXTRA, 128), F32)
    for k, row in enumerate(rows):
        tile = jnp.where(place == k, jnp.broadcast_to(row, (EXTRA, 128)), tile)
    return tile.astype(BF)


def kernel(
    q_hbm, k_hbm, v_hbm, o_hbm, og_hbm, w_hbm, seg_hbm,
    dq_in, dkv_in,
    qb, kb, vb, gb, og_own, ogb, ls_in, ls_out, w_ref, o_ref, seg_ref, segk, segq, kt, pb, mb, sh, lb, ga,
    gstage, dka, dva, dqt, dlt, dq_out, dkv_out,
    w_sem, o_sem, seg_sem, og_sem, own_sem, res_sem,
    q_s, q_r, k_s, k_r, v_s, v_r, g_s, g_r, og_s, og_r, ls_s, ls_r, dq_s, dq_r, dkv_s, dkv_r,
):
    seq = lax.axis_index("seq")
    head = lax.axis_index("head")
    y = seq // 16
    z = (seq // 2) % 8
    c = seq % 2
    ylo = head // 4
    x = head % 4
    sgn = 1 - 2 * ((z + c) % 2)

    def cols(other_head):
        h = 1 - c if other_head else c
        return pl.ds(pl.multiple_of(h * HD, HD), HD)

    def place(dy, steps, dc):
        yy = y + dy * (1 - 2 * y)
        return yy * 16 + ((z + 8 + sgn * steps) % 8) * 2 + (c + dc) % 2

    places_at = {(dy, steps, dc): place(dy, steps, dc) for dy in range(2) for steps in range(-5, 4) for dc in range(2)}

    def device(*where):
        return places_at[where] if all(isinstance(n, int) for n in where) else place(*where)

    def to_seq(src, dst, ssem, rsem, target):
        return pltpu.make_async_remote_copy(
            src_ref=src, dst_ref=dst, send_sem=ssem, recv_sem=rsem,
            device_id={"seq": target}, device_id_type=MESH)

    def to_head(src, dst, ssem, rsem, target):
        return pltpu.make_async_remote_copy(
            src_ref=src, dst_ref=dst, send_sem=ssem, recv_sem=rsem,
            device_id={"head": target}, device_id_type=MESH)

    local = [
        pltpu.make_async_copy(k_hbm.at[:, cols(0)], kb.at[0, 0, 0], own_sem.at[0]),
        pltpu.make_async_copy(q_hbm.at[:, cols(0)], qb.at[0, 0], own_sem.at[1]),
        pltpu.make_async_copy(v_hbm.at[:, cols(0)], vb.at[0, 0, 0], own_sem.at[2]),
        pltpu.make_async_copy(og_hbm, og_own, og_sem),
        pltpu.make_async_copy(o_hbm, o_ref, o_sem),
        pltpu.make_async_copy(w_hbm, w_ref, w_sem),
    ]
    seg_copy = pltpu.make_async_copy(seg_hbm, seg_ref, seg_sem)
    seg_copy.start()
    for copy in local:
        copy.start()

    barrier = pltpu.get_barrier_semaphore()
    for peer in SEQ_PEERS:
        pl.semaphore_signal(barrier, inc=1, device_id={"seq": device(*peer)}, device_id_type=MESH)
    for dy, dx in HEAD_PEERS:
        peer = ((ylo + dy) % 2) * 4 + (x + dx) % 4
        pl.semaphore_signal(barrier, inc=1, device_id={"head": peer}, device_id_type=MESH)
    pl.semaphore_wait(barrier, len(SEQ_PEERS) + len(HEAD_PEERS))

    sent = []

    def go(copy):
        copy.start()
        sent.append(copy)

    def spread_keys(src, buf, ss, rs):
        for dy, dz, cc in ((1, 0, 0), (1, 0, 1), (0, 1, 0), (0, 1, 1), (0, 0, 1)):
            steps = (-dz if cc else dz)
            at = (dy, dz, cc)
            go(to_seq(src.at[:, cols(cc)], buf.at[at], ss.at[at], rs.at[at], device(dy, steps, cc)))

    def arrived(buf, rs, *at):
        to_seq(buf.at[at], buf.at[at], rs.at[at], rs.at[at], seq).wait_recv()

    def keys_on(buf, ss, rs):
        for cc in range(2):
            arrived(buf, rs, 1, 0, cc)
            go(to_seq(buf.at[1, 0, cc], buf.at[1, 1, cc], ss.at[1, 1, cc], rs.at[1, 1, cc], device(0, 1, 0)))

    def spread_directly(src, buf, ss, rs, which):
        for dy, dz, cc in which:
            at = (dy, dz, cc)
            go(to_seq(src.at[:, cols(cc)], buf.at[at], ss.at[at], rs.at[at], device(dy, (-dz if cc else dz), cc)))

    def keys_arrived(buf, rs):
        for dy, dz, cc in ((0, 0, 1), (0, 1, 0), (0, 1, 1), (1, 1, 0), (1, 1, 1)):
            arrived(buf, rs, dy, dz, cc)

    heads_at = {(dy, dx): ((ylo + dy) % 2) * 4 + (x + dx) % 4 for dy in range(2) for dx in range(4)}

    def rows_copy(src, slot, k, part, dy, dx):
        return to_head(src, ogb.at[slot, PARTS[part]], og_s.at[k, part], og_r.at[slot, part], heads_at[dy, dx])

    def own_rows(part):
        return og_hbm.at[PARTS[part]]

    def rows_x(part):
        for dx in (2, 1, 3):
            go(rows_copy(own_rows(part), 4 - dx, dx, part, 0, dx))

    def rows_y(part):
        go(rows_copy(own_rows(part), 4, 4, part, 1, 0))

    def rows_arrived(slot, part):
        at = (slot, part)
        rows = ogb.at[slot, PARTS[part]]
        to_head(rows, rows, og_s.at[at], og_r.at[at], head).wait_recv()

    def rows_on_x():
        rows_arrived(4, 0)
        for dx in (2, 1, 3):
            go(rows_copy(ogb.at[4, PARTS[0]], 8 - dx, 4 + dx, 0, 0, dx))

    def rows_on_y():
        for dx in (1, 3, 2):
            rows_arrived(dx, 1)
            go(rows_copy(ogb.at[dx, PARTS[1]], 4 + dx, 4 + dx, 1, 1, 0))

    def queries_to(*distances):
        for d in distances:
            for cc in range(2):
                if cc or d:
                    go(to_seq(q_hbm.at[:, cols(cc)], qb.at[d, cc], q_s.at[d, cc], q_r.at[d, cc],
                              device(0, QUERY_STEPS[cc][d], cc)))

    rows_y(0)
    spread_directly(k_hbm, kb, k_s, k_r, KEY_SLOTS[1:])
    rows_x(1)
    rows_x(0)
    rows_y(1)
    queries_to(1, 0, 2, 3)
    spread_keys(v_hbm, vb, v_s, v_r)
    seg_copy.wait()

    for dy in range(2):
        for dz in range(2):
            for cc in range(2):
                row = seg_ref[pl.ds(device(dy, dz, cc), 1), :].astype(F32)
                segk[dy * 4 + dz * 2 + cc] = across(row)

    for pair in range(2):
        rows = [seg_ref[pl.ds(device(0, -(2 * pair + dd), cc), 1), :].astype(F32) for dd in range(2) for cc in range(2)]
        segq[pair] = jnp.broadcast_to(jnp.concatenate(rows, axis=1), (8, 512))

    def chunk(n):
        return n // 2, n % 2

    def blocks_arrived(buf, rs, pair, *lead):
        for dd in range(2):
            for cc in range(2):
                if dd or cc:
                    arrived(buf, rs, *lead, 2 * pair + dd, cc)
                else:
                    @pl.when(pair > 0)
                    def _():
                        arrived(buf, rs, *lead, 2 * pair, 0)

    def owner(d, cc):
        return device(0, -d, cc)

    def queries(pair):
        return qb[pl.ds(2 * pair, 2)].reshape(512, HD)

    mb[...] = jnp.full(mb.shape, FLOOR, F32)

    def scores(pair, dy):
        def one(dz, carry):
            n = 2 * dy + dz
            s = dot_nt(kb[dy, dz].reshape(256, HD), queries(pair))
            seg = segk[pl.ds(2 * n, 2)].reshape(256, 128)
            s = jnp.where(jnp.concatenate([seg] * 4, axis=1) == segq[pair][0:1], s, MASKED)
            pb[pair, pl.ds(pl.multiple_of(n * 256, 256), 256)] = s
            mb[pair] = jnp.maximum(mb[pair], jnp.max(s.reshape(32, 8, 512), axis=0))
            return carry

        lax.fori_loop(0, 2, one, 0)

    for copy in local[:3]:
        copy.wait()
    for at in ((0, 0, 1), (0, 1, 0), (0, 1, 1)):
        arrived(kb, k_r, *at)
    blocks_arrived(qb, q_r, 0)
    scores(0, 0)
    rows_on_x()
    rows_on_y()
    for cc in range(2):
        arrived(kb, k_r, 1, 0, cc)
        arrived(kb, k_r, 1, 1, cc)
    scores(0, 1)
    blocks_arrived(qb, q_r, 1)
    scores(1, 0)
    scores(1, 1)
    keys_on(vb, v_s, v_r)

    def share_copy(d, e):
        return to_seq(ls_out.at[d], ls_in.at[e, d], ls_s.at[d, e], ls_r.at[e, d], device(0, SHARE_STEPS[d][e], 0))

    def sums(pair):
        top = jnp.max(mb[pair], axis=0, keepdims=True)
        lb[...] = jnp.zeros(lb.shape, F32)

        def one(n, carry):
            part = pl.ds(pl.multiple_of(n * 256, 256), 256)
            p = jnp.exp2((pb[pair, part] - top) * (SCALE * LOG2E))
            pb[pair, part] = p
            lb[...] += jnp.sum(p.reshape(32, 8, 512), axis=0)
            return carry

        lax.fori_loop(0, 4, one, 0)
        total = jnp.sum(lb[...], axis=0, keepdims=True)
        mb[pair] = jnp.broadcast_to(top * SCALE, (8, 512))
        logs = jnp.where(total > 0.0, top * SCALE + jnp.log(jnp.maximum(total, 1e-37)), MASKED)
        for dd in range(2):
            d = 2 * pair + dd
            for cc in range(2):
                n = (dd * 2 + cc) * 128
                ls_out[d, cc:cc + 1] = logs[:, n:n + 128]
            for e in range(4):
                if e != d:
                    go(share_copy(d, e))

    sums(0)
    sums(1)
    for copy in local[3:]:
        copy.wait()

    acc = None
    for slot in (0, 4, 1, 3, 2, 5, 7, 6):
        block = heads_at[slot // 4, slot % 4]
        for part in range(2):
            if slot and (slot, part) not in ((4, 0), (1, 1), (2, 1), (3, 1)):
                rows_arrived(slot, part)
        rows = ogb[slot] if slot else og_own[...]
        term = dot_nt(rows, w_ref[:, pl.ds(pl.multiple_of(block * 512, 512), 512)])
        acc = term if acc is None else acc + term
    ga[...] = acc.astype(BF)
    for cc in range(2):
        grad = ga[:, cols(cc)]
        delta = jnp.sum((grad.astype(F32) * o_ref[:, cols(cc)].astype(F32)).T, axis=0, keepdims=True)
        gstage[cc, 0:TOK] = grad
        gstage[cc, TOK:ROWS] = stat_tile(pieces(delta, 2))

    def send_grad(*distances):
        for d in distances:
            for cc in range(2):
                if cc or d:
                    go(to_seq(gstage.at[cc], gb.at[d, cc], g_s.at[d, cc], g_r.at[d, cc],
                              device(0, QUERY_STEPS[cc][d], cc)))

    send_grad(1, 0)
    gb[0, 0] = gstage[0]
    send_grad(2, 3)
    for n, (dy, dz, cc) in enumerate(KEY_SLOTS):
        kt[:, n * 128:(n + 1) * 128] = kb[dy, dz, cc].astype(F32).T.astype(BF)
    dka[...] = jnp.zeros(dka.shape, F32)
    dva[...] = jnp.zeros(dva.shape, F32)
    keys_arrived(vb, v_r)
    log_sums = []
    for d in range(4):
        parts = [ls_out[d]]
        for e in range(4):
            if e != d:
                arrived(ls_in, ls_r, d, e)
                parts.append(ls_in[d, e])
        top = jnp.maximum(jnp.maximum(parts[0], parts[1]), jnp.maximum(parts[2], parts[3]))
        total = sum(jnp.exp(part - top) for part in parts)
        log_sums.append(top + jnp.log(total))
    for pair in range(2):
        row = jnp.concatenate([log_sums[2 * pair + dd][cc:cc + 1] for dd in range(2) for cc in range(2)], axis=1)
        sh[pair] = jnp.exp(mb[pair] - row)

    places = [(d, cc) for d in range(4) for cc in range(2)]

    def grad_step(i, carry):
        pair, n = i // 4, 3 - i % 4
        dy, dz = n // 2, n % 2

        @pl.when(n == 3)
        def _():
            blocks_arrived(gb, g_r, pair)
            dqt[...] = jnp.zeros(dqt.shape, F32)
            deltas = []
            for dd in range(2):
                for cc in range(2):
                    stats = gb[2 * pair + dd, cc, TOK:ROWS].astype(F32)
                    deltas.append(stats[0:1] + stats[1:2])
            dlt[...] = jnp.broadcast_to(jnp.concatenate(deltas, axis=1), (8, 512))

        quer = queries(pair)
        grad = gb[pl.ds(2 * pair, 2), :, 0:TOK].reshape(512, HD)
        part = pl.ds(pl.multiple_of(n * 256, 256), 256)
        p = pb[pair, part] * sh[pair][0:1]
        dva[part] += dot_nn(p.astype(BF), grad)
        dp = dot_nt(vb[dy, dz].reshape(256, HD), grad)
        ds = (p * (dp - dlt[0:1])).astype(BF)
        dka[part] += dot_nn(ds, quer)
        dqt[...] += dot_nn(kt[:, part], ds)

        @pl.when(pair == 1)
        def _():
            for cc in range(2):
                rows = pl.ds(pl.multiple_of(n * 256 + cc * 128, 128), 128)
                dkv_out[dy, dz, cc, 0] = (dka[rows] * SCALE).astype(BF)
                dkv_out[dy, dz, cc, 1] = dva[rows].astype(BF)
                if cc:
                    dkv_copy(dy, dz, 1).start()
                else:
                    @pl.when(n > 0)
                    def _():
                        dkv_copy(dy, dz, 0).start()

        @pl.when(n == 0)
        def _():
            for dd in (1, 0):
                d = 2 * pair + dd
                for cc in range(2):
                    k = (dd * 2 + cc) * 128
                    dq_out[d, cc] = dqt[:, k:k + 128].T.astype(BF)
                    if dd or cc:
                        dq_copy(d, cc).start()
                    else:
                        @pl.when(pair > 0)
                        def _():
                            dq_copy(d, 0).start()

        return carry

    def dq_copy(d, cc):
        return to_seq(dq_out.at[d, cc], dq_in.at[d, cc], dq_s.at[d, cc], dq_r.at[d, cc], owner(d, cc))

    def dkv_copy(dy, dz, cc):
        return to_seq(dkv_out.at[dy, dz, cc], dkv_in.at[dy, dz, cc], dkv_s.at[dy, dz, cc], dkv_r.at[dy, dz, cc],
                      device(dy, dz, cc))

    lax.fori_loop(0, 8, grad_step, 0)

    results = [
        pltpu.make_async_copy(dq_out.at[0, 0], dq_in.at[0, 0], res_sem.at[0]),
        pltpu.make_async_copy(dkv_out.at[0, 0, 0], dkv_in.at[0, 0, 0], res_sem.at[1]),
    ]
    for copy in results:
        copy.start()
    for copy in sent:
        copy.wait_send()
    for d, cc in places[1:]:
        dq_copy(d, cc).wait_send()
        arrived(dq_in, dq_r, d, cc)
    for at in KEY_SLOTS[1:]:
        dkv_copy(*at).wait_send()
        arrived(dkv_in, dkv_r, *at)
    for copy in results:
        copy.wait()


def deliver(dq_in, dkv_in, dq_ref, dk_ref, dv_ref):
    c = lax.axis_index("seq") % 2
    for cc in range(2):
        h = (c + cc) % 2
        cols = pl.ds(pl.multiple_of(h * HD, HD), HD)
        parts = [dq_in[d, cc].astype(F32) for d in range(4)]
        dq_ref[:, cols] = (((parts[0] + parts[1]) + (parts[2] + parts[3])) * SCALE).astype(BF)
        for a, ref in enumerate((dk_ref, dv_ref)):
            parts = [dkv_in[dy, dz, cc, a].astype(F32) for dy in range(2) for dz in range(2)]
            ref[:, cols] = ((parts[0] + parts[1]) + (parts[2] + parts[3])).astype(BF)


def shards(queries, keys, values, attn_out, out_grad, out_weight, segment_ids):
    anywhere = pl.BlockSpec(memory_space=pl.ANY)
    dma = pltpu.SemaphoreType.DMA
    vmem = pltpu.VMEM
    out = jax.ShapeDtypeStruct((TOK, 2 * HD), BF)
    query_sems = [dma((4, 2))] * 2
    key_sems = [dma((2, 2, 2))] * 2
    held = pl.pallas_call(
        kernel,
        out_shape=(
            jax.ShapeDtypeStruct((4, 2, TOK, HD), BF),
            jax.ShapeDtypeStruct((2, 2, 2, 2, TOK, HD), BF),
        ),
        in_specs=[anywhere] * 7,
        out_specs=(anywhere, anywhere),
        scratch_shapes=[
            vmem((4, 2, TOK, HD), BF),
            vmem((2, 2, 2, TOK, HD), BF),
            vmem((2, 2, 2, TOK, HD), BF),
            vmem((4, 2, ROWS, HD), BF),
            vmem((TOK, 512), BF),
            vmem((8, TOK, 512), BF),
            vmem((4, 4, 2, 128), F32),
            vmem((4, 2, 128), F32),
            vmem((256, 4096), BF),
            vmem((TOK, 2 * HD), BF),
            vmem((32, 128), jnp.int32),
            vmem((8, 128, 128), F32),
            vmem((2, 8, 512), F32),
            vmem((HD, 1024), BF),
            vmem((2, 1024, 512), F32),
            vmem((2, 8, 512), F32),
            vmem((2, 8, 512), F32),
            vmem((8, 512), F32),
            vmem((TOK, 2 * HD), BF),
            vmem((2, ROWS, HD), BF),
            vmem((1024, HD), F32),
            vmem((1024, HD), F32),
            vmem((HD, 512), F32),
            vmem((8, 512), F32),
            vmem((4, 2, TOK, HD), BF),
            vmem((2, 2, 2, 2, TOK, HD), BF),
            dma, dma, dma, dma, dma((3,)), dma((3,)),
            *query_sems, *key_sems, *key_sems, *query_sems, dma((8, 2)), dma((8, 2)), dma((4, 4)), dma((4, 4)),
            *query_sems, *key_sems,
        ],
        compiler_params=pltpu.CompilerParams(
            collective_id=0, has_side_effects=True, vmem_limit_bytes=60 * 1024 * 1024),
    )(queries, keys, values, attn_out, out_grad, out_weight, segment_ids.reshape(32, 128))
    return pl.pallas_call(
        deliver,
        out_shape=(out, out, out),
        in_specs=[pl.BlockSpec(memory_space=pltpu.VMEM)] * 2,
        out_specs=(pl.BlockSpec(memory_space=pltpu.VMEM),) * 3,
        name="deliver_call",
    )(*held)


def solution(mesh):
    return jax.shard_map(
        shards,
        mesh=mesh,
        in_specs=(
            P("seq", "head"),
            P("seq", "head"),
            P("seq", "head"),
            P("seq", "head"),
            P("seq", "head"),
            P("head", None),
            P(),
        ),
        out_specs=(P("seq", "head"), P("seq", "head"), P("seq", "head")),
        check_vma=False,
    )
```

```python
import jax
import jax.numpy as jnp
from jax import lax
from jax.experimental import pallas as pl
from jax.experimental.pallas import tpu as pltpu
from jax.sharding import PartitionSpec as P

HD = 128
TOK = 128
EXTRA = 16
SPLIT = 64
PARTS = (slice(0, SPLIT), slice(SPLIT, TOK))
ROWS = TOK + EXTRA
SCALE = HD ** -0.5
LOG2E = 1.4426950408889634
MASKED = -1e30
FLOOR = -1e29
MESH = pl.DeviceIdType.MESH
BF = jnp.bfloat16
F32 = jnp.float32

SEQ_PEERS = (
    (0, -1, 0), (0, 1, 0), (0, 2, 0), (0, -2, 0), (0, -3, 0), (0, 3, 0),
    (0, 0, 1), (0, 1, 1), (0, -1, 1), (0, 3, 1), (0, -3, 1), (0, -2, 1),
    (1, 0, 0), (1, 1, 0), (1, 0, 1), (1, 1, 1), (1, -1, 1),
)
NEAR_FIRST = (1, 0, 2, 3)
KEY_SLOTS = tuple((dy, dz, cc) for dy in range(2) for dz in range(2) for cc in range(2))
HEAD_PEERS = ((1, 0), (0, 1), (0, 2), (0, 3))
QUERY_STEPS = ((0, -1, 2, -3), (0, 1, -2, 3))
SHARE_STEPS = tuple(tuple(-d + QUERY_STEPS[d % 2][e] for e in range(4)) for d in range(4))


def dot_nt(a, b):
    return lax.dot_general(a, b, (((1,), (1,)), ((), ())), preferred_element_type=F32)


def dot_nn(a, b):
    return lax.dot_general(a, b, (((1,), (0,)), ((), ())), preferred_element_type=F32)


def across(row):
    return jnp.broadcast_to(row, (128, 128)).T


def pieces(x, count):
    out = []
    for _ in range(count):
        high = x.astype(BF).astype(F32)
        out.append(high)
        x = x - high
    return out


def stat_tile(rows):
    place = lax.broadcasted_iota(jnp.int32, (EXTRA, 128), 0)
    tile = jnp.zeros((EXTRA, 128), F32)
    for k, row in enumerate(rows):
        tile = jnp.where(place == k, jnp.broadcast_to(row, (EXTRA, 128)), tile)
    return tile.astype(BF)


def kernel(
    q_hbm, k_hbm, v_hbm, o_hbm, og_hbm, w_hbm, seg_hbm,
    dq_in, dkv_in,
    qb, kb, vb, gb, og_own, ogb, ls_in, ls_out, w_ref, o_ref, seg_ref, segk, segq, kt, pb, mb, sh, lb, acc, ga,
    gstage, dka, dva, dqt, dlt, dq_out, dkv_out,
    w_sem, o_sem, seg_sem, og_sem, own_sem, res_sem,
    q_s, q_r, k_s, k_r, v_s, v_r, g_s, g_r, og_s, og_r, ls_s, ls_r, dq_s, dq_r, dkv_s, dkv_r,
):
    seq = lax.axis_index("seq")
    head = lax.axis_index("head")
    y = seq // 16
    z = (seq // 2) % 8
    c = seq % 2
    ylo = head // 4
    x = head % 4
    sgn = 1 - 2 * ((z + c) % 2)

    def cols(other_head):
        h = 1 - c if other_head else c
        return pl.ds(pl.multiple_of(h * HD, HD), HD)

    def place(dy, steps, dc):
        yy = y + dy * (1 - 2 * y)
        return yy * 16 + ((z + 8 + sgn * steps) % 8) * 2 + (c + dc) % 2

    places_at = {(dy, steps, dc): place(dy, steps, dc) for dy in range(2) for steps in range(-5, 4) for dc in range(2)}

    def device(*where):
        return places_at[where] if all(isinstance(n, int) for n in where) else place(*where)

    def to_seq(src, dst, ssem, rsem, target):
        return pltpu.make_async_remote_copy(
            src_ref=src, dst_ref=dst, send_sem=ssem, recv_sem=rsem,
            device_id={"seq": target}, device_id_type=MESH)

    def to_head(src, dst, ssem, rsem, target):
        return pltpu.make_async_remote_copy(
            src_ref=src, dst_ref=dst, send_sem=ssem, recv_sem=rsem,
            device_id={"head": target}, device_id_type=MESH)

    local = [
        pltpu.make_async_copy(k_hbm.at[:, cols(0)], kb.at[0, 0, 0], own_sem.at[0]),
        pltpu.make_async_copy(q_hbm.at[:, cols(0)], qb.at[0, 0], own_sem.at[1]),
        pltpu.make_async_copy(v_hbm.at[:, cols(0)], vb.at[0, 0, 0], own_sem.at[2]),
        pltpu.make_async_copy(og_hbm, og_own, og_sem),
        pltpu.make_async_copy(o_hbm, o_ref, o_sem),
        pltpu.make_async_copy(w_hbm, w_ref, w_sem),
    ]
    seg_copy = pltpu.make_async_copy(seg_hbm, seg_ref, seg_sem)
    seg_copy.start()
    for copy in local:
        copy.start()

    barrier = pltpu.get_barrier_semaphore()
    for peer in SEQ_PEERS:
        pl.semaphore_signal(barrier, inc=1, device_id={"seq": device(*peer)}, device_id_type=MESH)
    for dy, dx in HEAD_PEERS:
        peer = ((ylo + dy) % 2) * 4 + (x + dx) % 4
        pl.semaphore_signal(barrier, inc=1, device_id={"head": peer}, device_id_type=MESH)
    pl.semaphore_wait(barrier, len(SEQ_PEERS) + len(HEAD_PEERS))

    sent = []

    def go(copy):
        copy.start()
        sent.append(copy)

    def spread_keys(src, buf, ss, rs):
        for dy, dz, cc in ((1, 0, 0), (1, 0, 1), (0, 1, 0), (0, 1, 1), (0, 0, 1)):
            steps = (-dz if cc else dz)
            at = (dy, dz, cc)
            go(to_seq(src.at[:, cols(cc)], buf.at[at], ss.at[at], rs.at[at], device(dy, steps, cc)))

    def arrived(buf, rs, *at):
        to_seq(buf.at[at], buf.at[at], rs.at[at], rs.at[at], seq).wait_recv()

    def keys_on(buf, ss, rs):
        for cc in range(2):
            arrived(buf, rs, 1, 0, cc)
            go(to_seq(buf.at[1, 0, cc], buf.at[1, 1, cc], ss.at[1, 1, cc], rs.at[1, 1, cc], device(0, 1, 0)))

    def spread_directly(src, buf, ss, rs, which):
        for dy, dz, cc in which:
            at = (dy, dz, cc)
            go(to_seq(src.at[:, cols(cc)], buf.at[at], ss.at[at], rs.at[at], device(dy, (-dz if cc else dz), cc)))

    def keys_arrived(buf, rs):
        for dy, dz, cc in ((0, 0, 1), (0, 1, 0), (0, 1, 1), (1, 1, 0), (1, 1, 1)):
            arrived(buf, rs, dy, dz, cc)

    heads_at = {(dy, dx): ((ylo + dy) % 2) * 4 + (x + dx) % 4 for dy in range(2) for dx in range(4)}

    def rows_copy(src, slot, k, part, dy, dx):
        return to_head(src, ogb.at[slot, PARTS[part]], og_s.at[k, part], og_r.at[slot, part], heads_at[dy, dx])

    def own_rows(part):
        return og_hbm.at[PARTS[part]]

    def rows_x(part):
        for dx in (2, 1, 3):
            go(rows_copy(own_rows(part), 4 - dx, dx, part, 0, dx))

    def rows_y(part):
        go(rows_copy(own_rows(part), 4, 4, part, 1, 0))

    def rows_arrived(slot, part):
        at = (slot, part)
        rows = ogb.at[slot, PARTS[part]]
        to_head(rows, rows, og_s.at[at], og_r.at[at], head).wait_recv()

    def rows_on_x():
        rows_arrived(4, 0)
        for dx in (2, 1, 3):
            go(rows_copy(ogb.at[4, PARTS[0]], 8 - dx, 4 + dx, 0, 0, dx))

    def rows_on_y():
        for dx in (1, 3, 2):
            rows_arrived(dx, 1)
            go(rows_copy(ogb.at[dx, PARTS[1]], 4 + dx, 4 + dx, 1, 1, 0))

    def queries_to(*distances):
        for d in distances:
            for cc in range(2):
                if cc or d:
                    go(to_seq(q_hbm.at[:, cols(cc)], qb.at[d, cc], q_s.at[d, cc], q_r.at[d, cc],
                              device(0, QUERY_STEPS[cc][d], cc)))

    rows_y(0)
    spread_directly(k_hbm, kb, k_s, k_r, KEY_SLOTS[1:])
    rows_x(1)
    rows_x(0)
    rows_y(1)
    queries_to(1, 0, 2, 3)
    spread_keys(v_hbm, vb, v_s, v_r)
    seg_copy.wait()

    for dy in range(2):
        for dz in range(2):
            for cc in range(2):
                row = seg_ref[pl.ds(device(dy, dz, cc), 1), :].astype(F32)
                segk[dy * 4 + dz * 2 + cc] = across(row)

    for pair in range(2):
        rows = [seg_ref[pl.ds(device(0, -(2 * pair + dd), cc), 1), :].astype(F32) for dd in range(2) for cc in range(2)]
        segq[pair] = jnp.broadcast_to(jnp.concatenate(rows, axis=1), (8, 512))

    def chunk(n):
        return n // 2, n % 2

    def blocks_arrived(buf, rs, pair, *lead):
        for dd in range(2):
            for cc in range(2):
                if dd or cc:
                    arrived(buf, rs, *lead, 2 * pair + dd, cc)
                else:
                    @pl.when(pair > 0)
                    def _():
                        arrived(buf, rs, *lead, 2 * pair, 0)

    def owner(d, cc):
        return device(0, -d, cc)

    def queries(pair):
        return qb[pl.ds(2 * pair, 2)].reshape(512, HD)

    mb[...] = jnp.full(mb.shape, FLOOR, F32)

    def scores(pair, dy):
        def one(dz, carry):
            n = 2 * dy + dz
            s = dot_nt(kb[dy, dz].reshape(256, HD), queries(pair))
            seg = segk[pl.ds(2 * n, 2)].reshape(256, 128)
            s = jnp.where(jnp.concatenate([seg] * 4, axis=1) == segq[pair][0:1], s, MASKED)
            pb[pair, pl.ds(pl.multiple_of(n * 256, 256), 256)] = s
            mb[pair] = jnp.maximum(mb[pair], jnp.max(s.reshape(32, 8, 512), axis=0))
            return carry

        lax.fori_loop(0, 2, one, 0)

    for copy in local[:3]:
        copy.wait()
    for at in ((0, 0, 1), (0, 1, 0), (0, 1, 1)):
        arrived(kb, k_r, *at)
    blocks_arrived(qb, q_r, 0)
    scores(0, 0)
    rows_on_x()
    rows_on_y()

    def share_copy(d, e):
        return to_seq(ls_out.at[d], ls_in.at[e, d], ls_s.at[d, e], ls_r.at[e, d], device(0, SHARE_STEPS[d][e], 0))

    def sums(pair):
        top = jnp.max(mb[pair], axis=0, keepdims=True)
        lb[...] = jnp.zeros(lb.shape, F32)

        def one(n, carry):
            part = pl.ds(pl.multiple_of(n * 256, 256), 256)
            p = jnp.exp2((pb[pair, part] - top) * (SCALE * LOG2E))
            pb[pair, part] = p
            lb[...] += jnp.sum(p.reshape(32, 8, 512), axis=0)
            return carry

        lax.fori_loop(0, 4, one, 0)
        total = jnp.sum(lb[...], axis=0, keepdims=True)
        mb[pair] = jnp.broadcast_to(top * SCALE, (8, 512))
        logs = jnp.where(total > 0.0, top * SCALE + jnp.log(jnp.maximum(total, 1e-37)), MASKED)
        for dd in range(2):
            d = 2 * pair + dd
            for cc in range(2):
                n = (dd * 2 + cc) * 128
                ls_out[d, cc:cc + 1] = logs[:, n:n + 128]
            for e in range(4):
                if e != d:
                    go(share_copy(d, e))

    def out_products(*slots):
        total = None
        for slot in slots:
            block = heads_at[slot // 4, slot % 4]
            for part in range(2):
                if slot and (slot, part) not in ((4, 0), (1, 1), (2, 1), (3, 1)):
                    rows_arrived(slot, part)
            rows = ogb[slot] if slot else og_own[...]
            term = dot_nt(rows, w_ref[:, pl.ds(pl.multiple_of(block * 512, 512), 512)])
            total = term if total is None else total + term
        return total

    for cc in range(2):
        arrived(kb, k_r, 1, 0, cc)
        arrived(kb, k_r, 1, 1, cc)
    scores(0, 1)
    sums(0)
    blocks_arrived(qb, q_r, 1)
    scores(1, 0)
    scores(1, 1)

    sums(1)
    keys_on(vb, v_s, v_r)
    for copy in local[3:]:
        copy.wait()
    acc[...] = out_products(0, 4, 1, 3, 2)
    ga[...] = (acc[...] + out_products(5, 7, 6)).astype(BF)
    for cc in range(2):
        grad = ga[:, cols(cc)]
        delta = jnp.sum((grad.astype(F32) * o_ref[:, cols(cc)].astype(F32)).T, axis=0, keepdims=True)
        gstage[cc, 0:TOK] = grad
        gstage[cc, TOK:ROWS] = stat_tile(pieces(delta, 2))

    def send_grad(*distances):
        for d in distances:
            for cc in range(2):
                if cc or d:
                    go(to_seq(gstage.at[cc], gb.at[d, cc], g_s.at[d, cc], g_r.at[d, cc],
                              device(0, QUERY_STEPS[cc][d], cc)))

    send_grad(1, 0)
    gb[0, 0] = gstage[0]
    send_grad(2, 3)
    for n, (dy, dz, cc) in enumerate(KEY_SLOTS):
        kt[:, n * 128:(n + 1) * 128] = kb[dy, dz, cc].astype(F32).T.astype(BF)
    dka[...] = jnp.zeros(dka.shape, F32)
    dva[...] = jnp.zeros(dva.shape, F32)
    keys_arrived(vb, v_r)
    log_sums = []
    for d in range(4):
        parts = [ls_out[d]]
        for e in range(4):
            if e != d:
                arrived(ls_in, ls_r, d, e)
                parts.append(ls_in[d, e])
        top = jnp.maximum(jnp.maximum(parts[0], parts[1]), jnp.maximum(parts[2], parts[3]))
        total = sum(jnp.exp(part - top) for part in parts)
        log_sums.append(top + jnp.log(total))
    for pair in range(2):
        row = jnp.concatenate([log_sums[2 * pair + dd][cc:cc + 1] for dd in range(2) for cc in range(2)], axis=1)
        sh[pair] = jnp.exp(mb[pair] - row)

    places = [(d, cc) for d in range(4) for cc in range(2)]

    def grad_step(i, carry):
        pair, n = i // 4, 3 - i % 4
        dy, dz = n // 2, n % 2

        @pl.when(n == 3)
        def _():
            blocks_arrived(gb, g_r, pair)
            dqt[...] = jnp.zeros(dqt.shape, F32)
            deltas = []
            for dd in range(2):
                for cc in range(2):
                    stats = gb[2 * pair + dd, cc, TOK:ROWS].astype(F32)
                    deltas.append(stats[0:1] + stats[1:2])
            dlt[...] = jnp.broadcast_to(jnp.concatenate(deltas, axis=1), (8, 512))

        quer = queries(pair)
        grad = gb[pl.ds(2 * pair, 2), :, 0:TOK].reshape(512, HD)
        part = pl.ds(pl.multiple_of(n * 256, 256), 256)
        p = pb[pair, part] * sh[pair][0:1]
        dva[part] += dot_nn(p.astype(BF), grad)
        dp = dot_nt(vb[dy, dz].reshape(256, HD), grad)
        ds = (p * (dp - dlt[0:1])).astype(BF)
        dka[part] += dot_nn(ds, quer)
        dqt[...] += dot_nn(kt[:, part], ds)

        @pl.when(pair == 1)
        def _():
            for cc in range(2):
                rows = pl.ds(pl.multiple_of(n * 256 + cc * 128, 128), 128)
                dkv_out[dy, dz, cc, 0] = (dka[rows] * SCALE).astype(BF)
                dkv_out[dy, dz, cc, 1] = dva[rows].astype(BF)
                if cc:
                    dkv_copy(dy, dz, 1).start()
                else:
                    @pl.when(n > 0)
                    def _():
                        dkv_copy(dy, dz, 0).start()

        @pl.when(n == 0)
        def _():
            for dd in (1, 0):
                d = 2 * pair + dd
                for cc in range(2):
                    k = (dd * 2 + cc) * 128
                    dq_out[d, cc] = dqt[:, k:k + 128].T.astype(BF)
                    if dd or cc:
                        dq_copy(d, cc).start()
                    else:
                        @pl.when(pair > 0)
                        def _():
                            dq_copy(d, 0).start()

        return carry

    def dq_copy(d, cc):
        return to_seq(dq_out.at[d, cc], dq_in.at[d, cc], dq_s.at[d, cc], dq_r.at[d, cc], owner(d, cc))

    def dkv_copy(dy, dz, cc):
        return to_seq(dkv_out.at[dy, dz, cc], dkv_in.at[dy, dz, cc], dkv_s.at[dy, dz, cc], dkv_r.at[dy, dz, cc],
                      device(dy, dz, cc))

    lax.fori_loop(0, 8, grad_step, 0)

    results = [
        pltpu.make_async_copy(dq_out.at[0, 0], dq_in.at[0, 0], res_sem.at[0]),
        pltpu.make_async_copy(dkv_out.at[0, 0, 0], dkv_in.at[0, 0, 0], res_sem.at[1]),
    ]
    for copy in results:
        copy.start()
    for copy in sent:
        copy.wait_send()
    for d, cc in places[1:]:
        dq_copy(d, cc).wait_send()
        arrived(dq_in, dq_r, d, cc)
    for at in KEY_SLOTS[1:]:
        dkv_copy(*at).wait_send()
        arrived(dkv_in, dkv_r, *at)
    for copy in results:
        copy.wait()


def deliver(dq_in, dkv_in, dq_ref, dk_ref, dv_ref, dq_parts, key_parts, outs, in_sem, out_sem):
    c = lax.axis_index("seq") % 2
    reads = [pltpu.make_async_copy(dq_in, dq_parts, in_sem.at[0])]
    reads += [pltpu.make_async_copy(dkv_in.at[:, :, :, a], key_parts.at[a], in_sem.at[1 + a]) for a in range(2)]
    writes = [pltpu.make_async_copy(outs.at[n], ref, out_sem.at[n]) for n, ref in enumerate((dq_ref, dk_ref, dv_ref))]
    for copy in reads:
        copy.start()
    for n in range(3):
        reads[n].wait()
        for cc in range(2):
            h = (c + cc) % 2
            if n:
                parts = [key_parts[n - 1, dy, dz, cc].astype(F32) for dy in range(2) for dz in range(2)]
            else:
                parts = [dq_parts[d, cc].astype(F32) for d in range(4)]
            total = (parts[0] + parts[1]) + (parts[2] + parts[3])
            outs[n, :, pl.ds(pl.multiple_of(h * HD, HD), HD)] = (total if n else total * SCALE).astype(BF)
        writes[n].start()
    for copy in writes:
        copy.wait()


def shards(queries, keys, values, attn_out, out_grad, out_weight, segment_ids):
    anywhere = pl.BlockSpec(memory_space=pl.ANY)
    dma = pltpu.SemaphoreType.DMA
    vmem = pltpu.VMEM
    out = jax.ShapeDtypeStruct((TOK, 2 * HD), BF)
    query_sems = [dma((4, 2))] * 2
    key_sems = [dma((2, 2, 2))] * 2
    held = pl.pallas_call(
        kernel,
        out_shape=(
            jax.ShapeDtypeStruct((4, 2, TOK, HD), BF),
            jax.ShapeDtypeStruct((2, 2, 2, 2, TOK, HD), BF),
        ),
        in_specs=[anywhere] * 7,
        out_specs=(anywhere, anywhere),
        scratch_shapes=[
            vmem((4, 2, TOK, HD), BF),
            vmem((2, 2, 2, TOK, HD), BF),
            vmem((2, 2, 2, TOK, HD), BF),
            vmem((4, 2, ROWS, HD), BF),
            vmem((TOK, 512), BF),
            vmem((8, TOK, 512), BF),
            vmem((4, 4, 2, 128), F32),
            vmem((4, 2, 128), F32),
            vmem((256, 4096), BF),
            vmem((TOK, 2 * HD), BF),
            vmem((32, 128), jnp.int32),
            vmem((8, 128, 128), F32),
            vmem((2, 8, 512), F32),
            vmem((HD, 1024), BF),
            vmem((2, 1024, 512), F32),
            vmem((2, 8, 512), F32),
            vmem((2, 8, 512), F32),
            vmem((8, 512), F32),
            vmem((TOK, 2 * HD), F32),
            vmem((TOK, 2 * HD), BF),
            vmem((2, ROWS, HD), BF),
            vmem((1024, HD), F32),
            vmem((1024, HD), F32),
            vmem((HD, 512), F32),
            vmem((8, 512), F32),
            vmem((4, 2, TOK, HD), BF),
            vmem((2, 2, 2, 2, TOK, HD), BF),
            dma, dma, dma, dma, dma((3,)), dma((3,)),
            *query_sems, *key_sems, *key_sems, *query_sems, dma((8, 2)), dma((8, 2)), dma((4, 4)), dma((4, 4)),
            *query_sems, *key_sems,
        ],
        compiler_params=pltpu.CompilerParams(
            collective_id=0, has_side_effects=True, vmem_limit_bytes=60 * 1024 * 1024),
    )(queries, keys, values, attn_out, out_grad, out_weight, segment_ids.reshape(32, 128))
    return pl.pallas_call(
        deliver,
        out_shape=(out, out, out),
        in_specs=[anywhere] * 2,
        out_specs=(anywhere, anywhere, anywhere),
        scratch_shapes=[
            vmem((4, 2, TOK, HD), BF),
            vmem((2, 2, 2, 2, TOK, HD), BF),
            vmem((3, TOK, 2 * HD), BF),
            dma((3,)), dma((3,)),
        ],
        compiler_params=pltpu.CompilerParams(vmem_limit_bytes=60 * 1024 * 1024),
        name="deliver_call",
    )(*held)


def solution(mesh):
    return jax.shard_map(
        shards,
        mesh=mesh,
        in_specs=(
            P("seq", "head"),
            P("seq", "head"),
            P("seq", "head"),
            P("seq", "head"),
            P("seq", "head"),
            P("head", None),
            P(),
        ),
        out_specs=(P("seq", "head"), P("seq", "head"), P("seq", "head")),
        check_vma=False,
    )
```

```python
import jax
import jax.numpy as jnp
from jax import lax
from jax.experimental import pallas as pl
from jax.experimental.pallas import tpu as pltpu
from jax.sharding import PartitionSpec as P

HD = 128
TOK = 128
EXTRA = 16
SPLIT = 64
PARTS = (slice(0, SPLIT), slice(SPLIT, TOK))
ROWS = TOK + EXTRA
SCALE = HD ** -0.5
LOG2E = 1.4426950408889634
MASKED = -1e30
FLOOR = -1e29
MESH = pl.DeviceIdType.MESH
BF = jnp.bfloat16
F32 = jnp.float32

SEQ_PEERS = (
    (0, -1, 0), (0, 1, 0), (0, 2, 0), (0, -2, 0), (0, -3, 0), (0, 3, 0),
    (0, 0, 1), (0, 1, 1), (0, -1, 1), (0, 3, 1), (0, -3, 1), (0, -2, 1),
    (1, 0, 0), (1, 1, 0), (1, 0, 1), (1, 1, 1), (1, -1, 1),
)
NEAR_FIRST = (1, 0, 2, 3)
KEY_SLOTS = tuple((dy, dz, cc) for dy in range(2) for dz in range(2) for cc in range(2))
HEAD_PEERS = ((1, 0), (0, 1), (0, 2), (0, 3))
QUERY_STEPS = ((0, -1, 2, -3), (0, 1, -2, 3))
SHARE_STEPS = tuple(tuple(-d + QUERY_STEPS[d % 2][e] for e in range(4)) for d in range(4))


def dot_nt(a, b):
    return lax.dot_general(a, b, (((1,), (1,)), ((), ())), preferred_element_type=F32)


def dot_nn(a, b):
    return lax.dot_general(a, b, (((1,), (0,)), ((), ())), preferred_element_type=F32)


def across(row):
    return jnp.broadcast_to(row, (128, 128)).T


def pieces(x, count):
    out = []
    for _ in range(count):
        high = x.astype(BF).astype(F32)
        out.append(high)
        x = x - high
    return out


def stat_tile(rows):
    place = lax.broadcasted_iota(jnp.int32, (EXTRA, 128), 0)
    tile = jnp.zeros((EXTRA, 128), F32)
    for k, row in enumerate(rows):
        tile = jnp.where(place == k, jnp.broadcast_to(row, (EXTRA, 128)), tile)
    return tile.astype(BF)


def kernel(
    q_hbm, k_hbm, v_hbm, o_hbm, og_hbm, w_hbm, seg_hbm,
    dq_in, dkv_in,
    qb, kb, vb, gb, og_own, ogb, ls_in, ls_out, w_ref, o_ref, seg_ref, segk, segq, kt, pb, mb, sh, lb, acc, ga,
    gstage, dka, dva, dqt, dlt, dq_out, dkv_out,
    w_sem, o_sem, seg_sem, og_sem, own_sem, res_sem,
    q_s, q_r, k_s, k_r, v_s, v_r, g_s, g_r, og_s, og_r, ls_s, ls_r, dq_s, dq_r, dkv_s, dkv_r,
):
    seq = lax.axis_index("seq")
    head = lax.axis_index("head")
    y = seq // 16
    z = (seq // 2) % 8
    c = seq % 2
    ylo = head // 4
    x = head % 4
    sgn = 1 - 2 * ((z + c) % 2)

    def cols(other_head):
        h = 1 - c if other_head else c
        return pl.ds(pl.multiple_of(h * HD, HD), HD)

    def place(dy, steps, dc):
        yy = y + dy * (1 - 2 * y)
        return yy * 16 + ((z + 8 + sgn * steps) % 8) * 2 + (c + dc) % 2

    places_at = {(dy, steps, dc): place(dy, steps, dc) for dy in range(2) for steps in range(-5, 4) for dc in range(2)}

    def device(*where):
        return places_at[where] if all(isinstance(n, int) for n in where) else place(*where)

    def to_seq(src, dst, ssem, rsem, target):
        return pltpu.make_async_remote_copy(
            src_ref=src, dst_ref=dst, send_sem=ssem, recv_sem=rsem,
            device_id={"seq": target}, device_id_type=MESH)

    def to_head(src, dst, ssem, rsem, target):
        return pltpu.make_async_remote_copy(
            src_ref=src, dst_ref=dst, send_sem=ssem, recv_sem=rsem,
            device_id={"head": target}, device_id_type=MESH)

    local = [
        pltpu.make_async_copy(k_hbm.at[:, cols(0)], kb.at[0, 0, 0], own_sem.at[0]),
        pltpu.make_async_copy(q_hbm.at[:, cols(0)], qb.at[0, 0], own_sem.at[1]),
        pltpu.make_async_copy(v_hbm.at[:, cols(0)], vb.at[0, 0, 0], own_sem.at[2]),
        pltpu.make_async_copy(og_hbm, og_own, og_sem),
        pltpu.make_async_copy(o_hbm, o_ref, o_sem),
        pltpu.make_async_copy(w_hbm, w_ref, w_sem),
    ]
    seg_copy = pltpu.make_async_copy(seg_hbm, seg_ref, seg_sem)
    seg_copy.start()
    for copy in local:
        copy.start()

    barrier = pltpu.get_barrier_semaphore()
    for peer in SEQ_PEERS:
        pl.semaphore_signal(barrier, inc=1, device_id={"seq": device(*peer)}, device_id_type=MESH)
    for dy, dx in HEAD_PEERS:
        peer = ((ylo + dy) % 2) * 4 + (x + dx) % 4
        pl.semaphore_signal(barrier, inc=1, device_id={"head": peer}, device_id_type=MESH)
    pl.semaphore_wait(barrier, len(SEQ_PEERS) + len(HEAD_PEERS))

    sent = []

    def go(copy):
        copy.start()
        sent.append(copy)

    def spread_keys(src, buf, ss, rs):
        for dy, dz, cc in ((1, 0, 0), (1, 0, 1), (0, 1, 0), (0, 1, 1), (0, 0, 1)):
            steps = (-dz if cc else dz)
            at = (dy, dz, cc)
            go(to_seq(src.at[:, cols(cc)], buf.at[at], ss.at[at], rs.at[at], device(dy, steps, cc)))

    def arrived(buf, rs, *at):
        to_seq(buf.at[at], buf.at[at], rs.at[at], rs.at[at], seq).wait_recv()

    def keys_on(buf, ss, rs):
        for cc in range(2):
            arrived(buf, rs, 1, 0, cc)
            go(to_seq(buf.at[1, 0, cc], buf.at[1, 1, cc], ss.at[1, 1, cc], rs.at[1, 1, cc], device(0, 1, 0)))

    def spread_directly(src, buf, ss, rs, which):
        for dy, dz, cc in which:
            at = (dy, dz, cc)
            go(to_seq(src.at[:, cols(cc)], buf.at[at], ss.at[at], rs.at[at], device(dy, (-dz if cc else dz), cc)))

    def keys_arrived(buf, rs):
        for dy, dz, cc in ((0, 0, 1), (0, 1, 0), (0, 1, 1), (1, 1, 0), (1, 1, 1)):
            arrived(buf, rs, dy, dz, cc)

    heads_at = {(dy, dx): ((ylo + dy) % 2) * 4 + (x + dx) % 4 for dy in range(2) for dx in range(4)}

    def rows_copy(src, slot, k, part, dy, dx):
        return to_head(src, ogb.at[slot, PARTS[part]], og_s.at[k, part], og_r.at[slot, part], heads_at[dy, dx])

    def own_rows(part):
        return og_hbm.at[PARTS[part]]

    def rows_x(part):
        for dx in (2, 1, 3):
            go(rows_copy(own_rows(part), 4 - dx, dx, part, 0, dx))

    def rows_y(part):
        go(rows_copy(own_rows(part), 4, 4, part, 1, 0))

    def rows_arrived(slot, part):
        at = (slot, part)
        rows = ogb.at[slot, PARTS[part]]
        to_head(rows, rows, og_s.at[at], og_r.at[at], head).wait_recv()

    def rows_on_x():
        rows_arrived(4, 0)
        for dx in (2, 1, 3):
            go(rows_copy(ogb.at[4, PARTS[0]], 8 - dx, 4 + dx, 0, 0, dx))

    def rows_on_y():
        for dx in (1, 3, 2):
            rows_arrived(dx, 1)
            go(rows_copy(ogb.at[dx, PARTS[1]], 4 + dx, 4 + dx, 1, 1, 0))

    def queries_to(*distances):
        for d in distances:
            for cc in range(2):
                if cc or d:
                    go(to_seq(q_hbm.at[:, cols(cc)], qb.at[d, cc], q_s.at[d, cc], q_r.at[d, cc],
                              device(0, QUERY_STEPS[cc][d], cc)))

    rows_y(0)
    spread_directly(k_hbm, kb, k_s, k_r, KEY_SLOTS[1:])
    rows_x(1)
    rows_x(0)
    rows_y(1)
    queries_to(1, 0, 2, 3)
    spread_keys(v_hbm, vb, v_s, v_r)
    seg_copy.wait()

    for dy in range(2):
        for dz in range(2):
            for cc in range(2):
                row = seg_ref[pl.ds(device(dy, dz, cc), 1), :].astype(F32)
                segk[dy * 4 + dz * 2 + cc] = across(row)

    for pair in range(2):
        rows = [seg_ref[pl.ds(device(0, -(2 * pair + dd), cc), 1), :].astype(F32) for dd in range(2) for cc in range(2)]
        segq[pair] = jnp.broadcast_to(jnp.concatenate(rows, axis=1), (8, 512))

    def chunk(n):
        return n // 2, n % 2

    def blocks_arrived(buf, rs, pair, *lead):
        for dd in range(2):
            for cc in range(2):
                if dd or cc:
                    arrived(buf, rs, *lead, 2 * pair + dd, cc)
                else:
                    @pl.when(pair > 0)
                    def _():
                        arrived(buf, rs, *lead, 2 * pair, 0)

    def owner(d, cc):
        return device(0, -d, cc)

    def queries(pair):
        return qb[pl.ds(2 * pair, 2)].reshape(512, HD)

    mb[...] = jnp.full(mb.shape, FLOOR, F32)

    def scores(pair, dy):
        def one(dz, carry):
            n = 2 * dy + dz
            s = dot_nt(kb[dy, dz].reshape(256, HD), queries(pair))
            seg = segk[pl.ds(2 * n, 2)].reshape(256, 128)
            s = jnp.where(jnp.concatenate([seg] * 4, axis=1) == segq[pair][0:1], s, MASKED)
            pb[pair, pl.ds(pl.multiple_of(n * 256, 256), 256)] = s
            mb[pair] = jnp.maximum(mb[pair], jnp.max(s.reshape(32, 8, 512), axis=0))
            return carry

        lax.fori_loop(0, 2, one, 0)

    for copy in local[:3]:
        copy.wait()
    for at in ((0, 0, 1), (0, 1, 0), (0, 1, 1)):
        arrived(kb, k_r, *at)
    blocks_arrived(qb, q_r, 0)
    scores(0, 0)
    rows_on_x()
    rows_on_y()

    def share_copy(d, e):
        return to_seq(ls_out.at[d], ls_in.at[e, d], ls_s.at[d, e], ls_r.at[e, d], device(0, SHARE_STEPS[d][e], 0))

    def sums(pair):
        top = jnp.max(mb[pair], axis=0, keepdims=True)
        lb[...] = jnp.zeros(lb.shape, F32)

        def one(n, carry):
            part = pl.ds(pl.multiple_of(n * 256, 256), 256)
            p = jnp.exp2((pb[pair, part] - top) * (SCALE * LOG2E))
            pb[pair, part] = p
            lb[...] += jnp.sum(p.reshape(32, 8, 512), axis=0)
            return carry

        lax.fori_loop(0, 4, one, 0)
        total = jnp.sum(lb[...], axis=0, keepdims=True)
        mb[pair] = jnp.broadcast_to(top * SCALE, (8, 512))
        logs = jnp.where(total > 0.0, top * SCALE + jnp.log(jnp.maximum(total, 1e-37)), MASKED)
        for dd in range(2):
            d = 2 * pair + dd
            for cc in range(2):
                n = (dd * 2 + cc) * 128
                ls_out[d, cc:cc + 1] = logs[:, n:n + 128]
            for e in range(4):
                if e != d:
                    go(share_copy(d, e))

    def out_products(*slots):
        total = None
        for slot in slots:
            block = heads_at[slot // 4, slot % 4]
            for part in range(2):
                if slot and (slot, part) not in ((4, 0), (1, 1), (2, 1), (3, 1)):
                    rows_arrived(slot, part)
            rows = ogb[slot] if slot else og_own[...]
            term = dot_nt(rows, w_ref[:, pl.ds(pl.multiple_of(block * 512, 512), 512)])
            total = term if total is None else total + term
        return total

    for cc in range(2):
        arrived(kb, k_r, 1, 0, cc)
        arrived(kb, k_r, 1, 1, cc)
    scores(0, 1)
    sums(0)
    for n, (dy, dz, cc) in enumerate(KEY_SLOTS):
        kt[:, n * 128:(n + 1) * 128] = kb[dy, dz, cc].astype(F32).T.astype(BF)
    blocks_arrived(qb, q_r, 1)
    scores(1, 0)
    scores(1, 1)

    sums(1)
    keys_on(vb, v_s, v_r)
    for copy in local[3:]:
        copy.wait()
    acc[...] = out_products(0, 4, 1, 3, 2)
    ga[...] = (acc[...] + out_products(5, 7, 6)).astype(BF)
    for cc in range(2):
        grad = ga[:, cols(cc)]
        delta = jnp.sum((grad.astype(F32) * o_ref[:, cols(cc)].astype(F32)).T, axis=0, keepdims=True)
        gstage[cc, 0:TOK] = grad
        gstage[cc, TOK:ROWS] = stat_tile(pieces(delta, 2))

    def send_grad(*distances):
        for d in distances:
            for cc in range(2):
                if cc or d:
                    go(to_seq(gstage.at[cc], gb.at[d, cc], g_s.at[d, cc], g_r.at[d, cc],
                              device(0, QUERY_STEPS[cc][d], cc)))

    send_grad(1, 0)
    gb[0, 0] = gstage[0]
    send_grad(2, 3)
    dka[...] = jnp.zeros(dka.shape, F32)
    dva[...] = jnp.zeros(dva.shape, F32)
    keys_arrived(vb, v_r)
    log_sums = []
    for d in range(4):
        parts = [ls_out[d]]
        for e in range(4):
            if e != d:
                arrived(ls_in, ls_r, d, e)
                parts.append(ls_in[d, e])
        top = jnp.maximum(jnp.maximum(parts[0], parts[1]), jnp.maximum(parts[2], parts[3]))
        total = sum(jnp.exp(part - top) for part in parts)
        log_sums.append(top + jnp.log(total))
    for pair in range(2):
        row = jnp.concatenate([log_sums[2 * pair + dd][cc:cc + 1] for dd in range(2) for cc in range(2)], axis=1)
        sh[pair] = jnp.exp(mb[pair] - row)

    places = [(d, cc) for d in range(4) for cc in range(2)]

    def grad_step(i, carry):
        pair, n = i // 4, 3 - i % 4
        dy, dz = n // 2, n % 2

        @pl.when(n == 3)
        def _():
            blocks_arrived(gb, g_r, pair)
            dqt[...] = jnp.zeros(dqt.shape, F32)
            deltas = []
            for dd in range(2):
                for cc in range(2):
                    stats = gb[2 * pair + dd, cc, TOK:ROWS].astype(F32)
                    deltas.append(stats[0:1] + stats[1:2])
            dlt[...] = jnp.broadcast_to(jnp.concatenate(deltas, axis=1), (8, 512))

        quer = queries(pair)
        grad = gb[pl.ds(2 * pair, 2), :, 0:TOK].reshape(512, HD)
        part = pl.ds(pl.multiple_of(n * 256, 256), 256)
        p = pb[pair, part] * sh[pair][0:1]
        dva[part] += dot_nn(p.astype(BF), grad)
        dp = dot_nt(vb[dy, dz].reshape(256, HD), grad)
        ds = (p * (dp - dlt[0:1])).astype(BF)
        dka[part] += dot_nn(ds, quer)
        dqt[...] += dot_nn(kt[:, part], ds)

        @pl.when(pair == 1)
        def _():
            for cc in range(2):
                rows = pl.ds(pl.multiple_of(n * 256 + cc * 128, 128), 128)
                dkv_out[dy, dz, cc, 0] = (dka[rows] * SCALE).astype(BF)
                dkv_out[dy, dz, cc, 1] = dva[rows].astype(BF)
                if cc:
                    dkv_copy(dy, dz, 1).start()
                else:
                    @pl.when(n > 0)
                    def _():
                        dkv_copy(dy, dz, 0).start()

        @pl.when(n == 0)
        def _():
            for dd in (1, 0):
                d = 2 * pair + dd
                for cc in range(2):
                    k = (dd * 2 + cc) * 128
                    dq_out[d, cc] = dqt[:, k:k + 128].T.astype(BF)
                    if dd or cc:
                        dq_copy(d, cc).start()
                    else:
                        @pl.when(pair > 0)
                        def _():
                            dq_copy(d, 0).start()

        return carry

    def dq_copy(d, cc):
        return to_seq(dq_out.at[d, cc], dq_in.at[d, cc], dq_s.at[d, cc], dq_r.at[d, cc], owner(d, cc))

    def dkv_copy(dy, dz, cc):
        return to_seq(dkv_out.at[dy, dz, cc], dkv_in.at[dy, dz, cc], dkv_s.at[dy, dz, cc], dkv_r.at[dy, dz, cc],
                      device(dy, dz, cc))

    lax.fori_loop(0, 8, grad_step, 0)

    results = [
        pltpu.make_async_copy(dq_out.at[0, 0], dq_in.at[0, 0], res_sem.at[0]),
        pltpu.make_async_copy(dkv_out.at[0, 0, 0], dkv_in.at[0, 0, 0], res_sem.at[1]),
    ]
    for copy in results:
        copy.start()
    for copy in sent:
        copy.wait_send()
    for d, cc in places[1:]:
        dq_copy(d, cc).wait_send()
        arrived(dq_in, dq_r, d, cc)
    for at in KEY_SLOTS[1:]:
        dkv_copy(*at).wait_send()
        arrived(dkv_in, dkv_r, *at)
    for copy in results:
        copy.wait()


def deliver(dq_in, dkv_in, dq_ref, dk_ref, dv_ref, dq_parts, key_parts, outs, in_sem, out_sem):
    c = lax.axis_index("seq") % 2
    reads = [pltpu.make_async_copy(dq_in, dq_parts, in_sem.at[0])]
    reads += [pltpu.make_async_copy(dkv_in.at[:, :, :, a], key_parts.at[a], in_sem.at[1 + a]) for a in range(2)]
    writes = [pltpu.make_async_copy(outs.at[n], ref, out_sem.at[n]) for n, ref in enumerate((dq_ref, dk_ref, dv_ref))]
    for copy in reads:
        copy.start()
    for n in range(3):
        reads[n].wait()
        for cc in range(2):
            h = (c + cc) % 2
            if n:
                parts = [key_parts[n - 1, dy, dz, cc].astype(F32) for dy in range(2) for dz in range(2)]
            else:
                parts = [dq_parts[d, cc].astype(F32) for d in range(4)]
            total = (parts[0] + parts[1]) + (parts[2] + parts[3])
            outs[n, :, pl.ds(pl.multiple_of(h * HD, HD), HD)] = (total if n else total * SCALE).astype(BF)
        writes[n].start()
    for copy in writes:
        copy.wait()


def shards(queries, keys, values, attn_out, out_grad, out_weight, segment_ids):
    anywhere = pl.BlockSpec(memory_space=pl.ANY)
    dma = pltpu.SemaphoreType.DMA
    vmem = pltpu.VMEM
    out = jax.ShapeDtypeStruct((TOK, 2 * HD), BF)
    query_sems = [dma((4, 2))] * 2
    key_sems = [dma((2, 2, 2))] * 2
    held = pl.pallas_call(
        kernel,
        out_shape=(
            jax.ShapeDtypeStruct((4, 2, TOK, HD), BF),
            jax.ShapeDtypeStruct((2, 2, 2, 2, TOK, HD), BF),
        ),
        in_specs=[anywhere] * 7,
        out_specs=(anywhere, anywhere),
        scratch_shapes=[
            vmem((4, 2, TOK, HD), BF),
            vmem((2, 2, 2, TOK, HD), BF),
            vmem((2, 2, 2, TOK, HD), BF),
            vmem((4, 2, ROWS, HD), BF),
            vmem((TOK, 512), BF),
            vmem((8, TOK, 512), BF),
            vmem((4, 4, 2, 128), F32),
            vmem((4, 2, 128), F32),
            vmem((256, 4096), BF),
            vmem((TOK, 2 * HD), BF),
            vmem((32, 128), jnp.int32),
            vmem((8, 128, 128), F32),
            vmem((2, 8, 512), F32),
            vmem((HD, 1024), BF),
            vmem((2, 1024, 512), F32),
            vmem((2, 8, 512), F32),
            vmem((2, 8, 512), F32),
            vmem((8, 512), F32),
            vmem((TOK, 2 * HD), F32),
            vmem((TOK, 2 * HD), BF),
            vmem((2, ROWS, HD), BF),
            vmem((1024, HD), F32),
            vmem((1024, HD), F32),
            vmem((HD, 512), F32),
            vmem((8, 512), F32),
            vmem((4, 2, TOK, HD), BF),
            vmem((2, 2, 2, 2, TOK, HD), BF),
            dma, dma, dma, dma, dma((3,)), dma((3,)),
            *query_sems, *key_sems, *key_sems, *query_sems, dma((8, 2)), dma((8, 2)), dma((4, 4)), dma((4, 4)),
            *query_sems, *key_sems,
        ],
        compiler_params=pltpu.CompilerParams(
            collective_id=0, has_side_effects=True, vmem_limit_bytes=60 * 1024 * 1024),
    )(queries, keys, values, attn_out, out_grad, out_weight, segment_ids.reshape(32, 128))
    return pl.pallas_call(
        deliver,
        out_shape=(out, out, out),
        in_specs=[anywhere] * 2,
        out_specs=(anywhere, anywhere, anywhere),
        scratch_shapes=[
            vmem((4, 2, TOK, HD), BF),
            vmem((2, 2, 2, 2, TOK, HD), BF),
            vmem((3, TOK, 2 * HD), BF),
            dma((3,)), dma((3,)),
        ],
        compiler_params=pltpu.CompilerParams(vmem_limit_bytes=60 * 1024 * 1024),
        name="deliver_call",
    )(*held)


def solution(mesh):
    return jax.shard_map(
        shards,
        mesh=mesh,
        in_specs=(
            P("seq", "head"),
            P("seq", "head"),
            P("seq", "head"),
            P("seq", "head"),
            P("seq", "head"),
            P("head", None),
            P(),
        ),
        out_specs=(P("seq", "head"), P("seq", "head"), P("seq", "head")),
        check_vma=False,
    )
```
